512 devices in a mesh: grp: 16 (over z), blk: 32 (over y, x, core).
Axes of the slice: x: 4, y: 4, z: 16, core: 2. Of those that a mesh axis runs over, the one named last changes fastest.
Arguments:
- right_side: float32 [4, 131072, 128], P(None, ('grp', 'blk')), may hold values from -6 to 6
- inverse_diag: bfloat16 [131072, 256], P(('grp', 'blk'))
- factor_blocks: bfloat16 [512, 24, 256, 256], P(('grp', 'blk')), may hold values from -0.078125 to 0.078125
- sources: int32 [512, 24], P(('grp', 'blk')), may hold values from 0 to 31, as said below
- counts: int32 [512], P(('grp', 'blk')), may hold values from 1 to 24, as said below
- carry_in: float32 [131072, 128], P(('grp', 'blk')), may hold values from -6 to 6
Outputs:
- solved: float32 [4, 131072, 128], P(None, ('grp', 'blk'))
- carry_out: float32 [131072, 128], P(('grp', 'blk'))
The draws below stay inside these ranges and needn't reach their ends.
Inputs may be any that keep to these rules, and one draw needn't show every extreme that they name: Slots at or beyond counts[d] take no part; some row block uses all 24 slots. `sources`: slot 0 of row block d reads the opposite block of its group, (b + 32 / 2) modulo 32; every other slot reads a block that differs from d's own block index b by at most 3, counted cyclically within the group of 32 blocks.
All inputs are finite; a program needn't handle non-finite values.
Results may differ from the reference program's by a relative error of at most 0.009.
Values may be sent and summed in bfloat16 or wider, within the bound.
No kernel may reach another device: no remote copies, remote signals or barrier semaphores. Data moves between devices by JAX's collectives and lax.ppermute only.
A program may use at most 64 MiB of HBM per device.

```python
import math
import jax
import jax.numpy as jnp
from jax import lax

BLOCK = 256
COLS = 128
K_MAX = 24
REACH = 3
TICKS = 4
DEVS = 512
ROWS = 131072
N_GRP = 16
N_BLK = 32


def draw_inverse_diag(key, part):
    key = jax.random.fold_in(key, 11)
    key_lower, key_diag = jax.random.split(key)
    row_index = lax.broadcasted_iota(jnp.int32, (ROWS, BLOCK), 0) % BLOCK
    col_index = lax.broadcasted_iota(jnp.int32, (ROWS, BLOCK), 1)
    lower = jax.random.normal(key_lower, (ROWS, BLOCK), jnp.float32) * (1.2 / math.sqrt(BLOCK))
    diagonal = jnp.exp(jax.random.uniform(key_diag, (ROWS, BLOCK), jnp.float32, math.log(0.5), math.log(2.0)))
    values = jnp.where(col_index < row_index, lower, jnp.where(col_index == row_index, diagonal, 0.0))
    return values.astype(jnp.bfloat16)


def draw_sources(key, part):
    key = jax.random.fold_in(key, 31)
    offsets = jax.random.randint(key, (DEVS, K_MAX), -REACH, REACH + 1, jnp.int32)
    slot_index = lax.broadcasted_iota(jnp.int32, (DEVS, K_MAX), 1)
    offsets = jnp.where(slot_index == 0, N_BLK // 2, offsets)
    own_block = (jnp.arange(DEVS, dtype=jnp.int32) % N_BLK)[:, None]
    return ((own_block + offsets) % N_BLK).astype(jnp.int32)


def draw_counts(key, part):
    key = jax.random.fold_in(key, 23)
    key_first, key_second, key_full = jax.random.split(key, 3)
    first_draw = jax.random.randint(key_first, (DEVS,), 1, K_MAX + 1, jnp.int32)
    second_draw = jax.random.randint(key_second, (DEVS,), 1, K_MAX + 1, jnp.int32)
    full_index = jax.random.randint(key_full, (), 0, DEVS, jnp.int32)
    positions = jnp.arange(DEVS, dtype=jnp.int32)
    return jnp.where(positions == full_index, K_MAX, jnp.minimum(first_draw, second_draw)).astype(jnp.int32)


def levels(key, shape, cuts, least, top_value):
    gain = 1.0
    for position, shards_of in cuts:
        steps = jax.random.uniform(jax.random.fold_in(jax.random.fold_in(key, 6), position), (shards_of,), jnp.float32, least / len(cuts), top_value / len(cuts))
        gain = gain * jnp.repeat(jnp.exp(steps), shape[position] // shards_of).reshape((-1,) + (1,) * (len(shape) - 1 - position))
    return gain


def centred(rng, extent, deviation, most, pieces=(), kind=jnp.bfloat16):
    factor_of = levels(rng, extent, pieces, -0.22, 0.18) if pieces else 1.0
    entries = jax.random.normal(rng, extent, jnp.float32) * deviation * factor_of
    return jnp.minimum(jnp.maximum(entries, -most), most).astype(kind)


def setup_inputs(seed: int = 0) -> dict:
    key_of = jax.random.split(jax.random.key(seed), 7)
    right_side = centred(key_of[0], (TICKS, ROWS, COLS), 1.0, 6.0, ((1, 512),), jnp.float32)
    inverse_diag = draw_inverse_diag(jax.random.fold_in(key_of[6], 71), 0)
    factor_blocks = centred(key_of[2], (DEVS, K_MAX, BLOCK, BLOCK), (BLOCK * K_MAX) ** -0.5, 0.078125, ((0, 512),))
    sources = draw_sources(jax.random.fold_in(key_of[6], 71), 0)
    counts = draw_counts(jax.random.fold_in(key_of[6], 71), 0)
    carry_in = centred(key_of[5], (ROWS, COLS), 1.0, 6.0, ((0, 512),), jnp.float32)
    return dict(right_side=right_side, inverse_diag=inverse_diag, factor_blocks=factor_blocks, sources=sources, counts=counts, carry_in=carry_in)


def device_partial(factor_blocks, sources, counts, outgoing):
    def one_block(d):
        group_rows = lax.dynamic_index_in_dim(outgoing, d // N_BLK, 0, keepdims=False)

        def add_slot(k, running):
            matrix = lax.dynamic_index_in_dim(factor_blocks[d], k, 0, keepdims=False)
            start = (sources[d, k] * BLOCK).astype(jnp.int32)
            block_piece = lax.dynamic_slice_in_dim(group_rows, start, BLOCK, 0)
            return running + jnp.dot(matrix, block_piece, preferred_element_type=jnp.float32)

        return lax.fori_loop(jnp.int32(0), counts[d], add_slot, jnp.zeros((BLOCK, COLS), jnp.float32))

    return lax.map(one_block, jnp.arange(N_GRP * N_BLK, dtype=jnp.int32))


def reference(right_side, inverse_diag, factor_blocks, sources, counts, carry_in):
    blocks_all = N_GRP * N_BLK
    inverse = inverse_diag.reshape(blocks_all, BLOCK, BLOCK).astype(jnp.float32)
    incoming = carry_in.reshape(blocks_all, BLOCK, COLS)
    solved_ticks = []
    partial_value = incoming
    for tick_index in range(TICKS):
        residual = (right_side[tick_index].reshape(blocks_all, BLOCK, COLS) - incoming).astype(jnp.bfloat16)
        solved = jnp.einsum("dij,djc->dic", inverse, residual.astype(jnp.float32))
        solved_ticks.append(solved.reshape(ROWS, COLS))
        outgoing = solved.astype(jnp.bfloat16).reshape(N_GRP, N_BLK * BLOCK, COLS)
        partial_value = device_partial(factor_blocks, sources, counts, outgoing)
        grouped = partial_value.reshape(N_GRP, N_BLK, BLOCK, COLS)
        shifted = jnp.concatenate([jnp.zeros((1, N_BLK, BLOCK, COLS), jnp.float32), grouped[:-1]], axis=0)
        incoming = shifted.reshape(blocks_all, BLOCK, COLS)
    return jnp.stack(solved_ticks), partial_value.reshape(ROWS, COLS)
```

```python
import functools

import jax
import jax.numpy as jnp
from jax import lax
from jax.experimental import pallas as pl
from jax.experimental.pallas import tpu as pltpu
from jax.sharding import PartitionSpec as P

F32 = jnp.float32
BF16 = jnp.bfloat16
VMEM = pl.BlockSpec(memory_space=pltpu.VMEM)
SMEM = pl.BlockSpec(memory_space=pltpu.SMEM)
ANY = pl.BlockSpec(memory_space=pl.ANY)
LIMIT = 20 * 1024 * 1024


def params():
    return pltpu.CompilerParams(vmem_limit_bytes=LIMIT)


def mm(a, b):
    return jnp.dot(a, b, preferred_element_type=F32)


def combine_kernel(place, source_list, count, blocks, inverse, right, kept, handed, landing, sums, arrived):
    block = inverse.shape[0]
    live = count[0]
    own, sign, around = place[0], place[1], place[2]

    def copy_of(k):
        return pltpu.make_async_copy(blocks.at[0, k], landing.at[k], arrived.at[k])

    def begin(k, carry):
        copy_of(k).start()
        return carry

    lax.fori_loop(0, live, begin, 0)
    sums[...] = jnp.zeros_like(sums)
    handed[3 * block : 4 * block, :] = inverse[...]
    for tick in range(1, right.shape[0]):
        value = right[tick]
        high = value.astype(BF16)
        rows = pl.ds((3 + tick) * block, block)
        handed[rows, 0 : value.shape[1]] = high
        handed[rows, value.shape[1] :] = (value - high.astype(F32)).astype(BF16)

    def add(k, carry):
        copy_of(k).wait()
        offset = lax.rem(source_list[0, k] - own + 3 + around, around) - 3
        turned = offset * sign
        slot = jnp.where(k == 0, 4, jnp.where(turned >= 0, 3 - turned, 8 + turned))
        sums[slot] = sums[slot] + landing[k].astype(F32)
        return carry

    lax.fori_loop(0, live, add, 0)
    for i in range(5):
        kept[i] = sums[i].astype(BF16)
    for i in range(3):
        handed[i * block : (i + 1) * block, :] = sums[5 + i].astype(BF16)


def combine(place, sources, counts, factor_blocks, inverse_diag, right_side):
    slots, block = factor_blocks.shape[1], factor_blocks.shape[2]
    ticks = right_side.shape[0]
    return pl.pallas_call(
        combine_kernel,
        out_shape=(
            jax.ShapeDtypeStruct((5, block, block), BF16),
            jax.ShapeDtypeStruct(((3 + ticks) * block, block), BF16),
        ),
        in_specs=[SMEM, SMEM, SMEM, ANY, VMEM, VMEM],
        out_specs=(VMEM, VMEM),
        scratch_shapes=[
            pltpu.VMEM((slots, block, block), BF16),
            pltpu.VMEM((8, block, block), F32),
            pltpu.SemaphoreType.DMA((slots,)),
        ],
        compiler_params=params(),
        cost_estimate=pl.CostEstimate(flops=4_000_000, bytes_accessed=10_000_000, transcendentals=0),
        name="combine",
    )(place, sources, counts, factor_blocks, inverse_diag, right_side)


def first_kernel(right, incoming, inverse, solved, outgoing):
    value = mm(inverse[...], (right[0] - incoming[...]).astype(BF16))
    solved[...] = value
    outgoing[...] = value.astype(BF16)


def first_solve(right_side, carry_in, inverse_diag):
    ticks, block, columns = right_side.shape
    return pl.pallas_call(
        first_kernel,
        grid=(1,),
        out_shape=(
            jax.ShapeDtypeStruct((block, columns), F32),
            jax.ShapeDtypeStruct((block, columns), BF16),
        ),
        in_specs=[
            pl.BlockSpec((1, block, columns), lambda i: (0, 0, 0)),
            pl.BlockSpec((block, columns), lambda i: (0, 0)),
            pl.BlockSpec((block, block), lambda i: (0, 0)),
        ],
        out_specs=(
            pl.BlockSpec((block, columns), lambda i: (0, 0)),
            pl.BlockSpec((block, columns), lambda i: (0, 0)),
        ),
        compiler_params=params(),
        name="first",
    )(right_side, carry_in, inverse_diag)


def pair_kernel(tick, place, both, right, inverse, given, solved, outgoing):
    block, columns = solved.shape
    mine = place[3] * (2 * block)
    theirs = (1 - place[3]) * (2 * block)

    def part(at):
        return both[pl.ds(pl.multiple_of(at, block), block), :].astype(F32)

    incoming = part(mine) + part(theirs + block)
    other = part(mine + block) + part(theirs)
    value = mm(inverse[...], (right[tick] - incoming).astype(BF16))
    solved[...] = value
    outgoing[0:block] = value.astype(BF16)
    rows = pl.ds((3 + tick) * block, block)
    other_right = given[rows, 0:columns].astype(F32) + given[rows, columns:].astype(F32)
    value = mm(given[3 * block : 4 * block, :], (other_right - other).astype(BF16))
    outgoing[block:] = value.astype(BF16)


def pair_solve(tick, place, both, right_side, inverse_diag, given):
    ticks, block, columns = right_side.shape
    return pl.pallas_call(
        functools.partial(pair_kernel, tick),
        out_shape=(
            jax.ShapeDtypeStruct((block, columns), F32),
            jax.ShapeDtypeStruct((2 * block, columns), BF16),
        ),
        in_specs=[SMEM, VMEM, VMEM, VMEM, VMEM],
        out_specs=(VMEM, VMEM),
        compiler_params=params(),
        name="solve",
    )(place, both, right_side, inverse_diag, given)


def partial_kernel(place, kept, given, own, beside, third, opposite, sums, mine_exact):
    block = own.shape[0] // 2
    near = place[4] * (2 * block)

    def part(at):
        return beside[pl.ds(pl.multiple_of(at, block), block), :]

    odd_one, same_one = part(near), part(near + block)
    self_one = own[0:block]
    value = mm(kept[3], self_one)
    value += mm(kept[1], same_one)
    value += mm(kept[2], odd_one)
    value += mm(kept[0], third[...])
    value += mm(kept[4], opposite[...])
    other = mm(given[0:block, :], same_one)
    other += mm(given[block : 2 * block, :], odd_one)
    other += mm(given[2 * block : 3 * block, :], self_one)
    if mine_exact is not None:
        mine_exact[...] = value
        sums[...] = other.astype(BF16)
    else:
        sums[0:block] = value.astype(BF16)
        sums[block:] = other.astype(BF16)


def moving_kernel(place, kept, given, own, beside, third, opposite, sums):
    partial_kernel(place, kept, given, own, beside, third, opposite, sums, None)


def partial_sums(place, kept, given, own, beside, third, opposite, last):
    block, columns = third.shape
    if last:
        kernel = partial_kernel
        shapes = (
            jax.ShapeDtypeStruct((block, columns), BF16),
            jax.ShapeDtypeStruct((block, columns), F32),
        )
        specs = (VMEM, VMEM)
    else:
        kernel = moving_kernel
        shapes = jax.ShapeDtypeStruct((2 * block, columns), BF16)
        specs = VMEM
    return pl.pallas_call(
        kernel,
        out_shape=shapes,
        in_specs=[SMEM, VMEM, VMEM, VMEM, VMEM, VMEM, VMEM],
        out_specs=specs,
        compiler_params=params(),
        name="partial",
    )(place, kept, given, own, beside, third, opposite)


def carry_kernel(place, exact, both, carry):
    block = exact.shape[0]
    theirs = pl.multiple_of((1 - place[3]) * block, block)
    carry[...] = exact[...] + both[pl.ds(theirs, block), :].astype(F32)


def carry_sum(place, exact, both):
    return pl.pallas_call(
        carry_kernel,
        out_shape=jax.ShapeDtypeStruct(exact.shape, F32),
        in_specs=[SMEM, VMEM, VMEM],
        out_specs=VMEM,
        compiler_params=params(),
        name="carry",
    )(place, exact, both)


def shards(right_side, inverse_diag, factor_blocks, sources, counts, carry_in):
    ticks = right_side.shape[0]
    groups, around = lax.axis_size("grp"), lax.axis_size("blk")
    chips = around // 2
    at = lax.axis_index("blk").astype(jnp.int32)
    odd = lax.rem(at, 2)
    place = jnp.stack([at, 2 * odd - 1, jnp.int32(around), odd, odd])

    chip_pairs = [[2 * c, 2 * c + 1] for c in range(chips)]
    next_pairs = [[2 * c + 1, (2 * c + 2) % around] for c in range(chips)]
    third_of = [(2 * c + 1, (2 * c + 4) % around) for c in range(chips)]
    third_of = third_of + [(b, a) for a, b in third_of]
    opposite_of = [(b, (b + around // 2) % around) for b in range(around)]

    def paired(value, pairs):
        return lax.all_gather(value, "blk", axis=0, tiled=True, axis_index_groups=pairs)

    solved_ticks = []
    solved, first = first_solve(right_side, carry_in, inverse_diag)
    solved_ticks.append(solved)
    kept, handed = combine(place, sources, counts, factor_blocks, inverse_diag, right_side)
    given = lax.ppermute(handed, "blk", [(b, b ^ 1) for b in range(around)])
    carry = None
    for tick in range(ticks):
        if tick == 0:
            mine = first
            chip = paired(first, chip_pairs)
            own = jnp.where(odd == 0, chip, jnp.roll(chip, chip.shape[0] // 2, 0))
        else:
            mine = own[0 : own.shape[0] // 2]
        third = lax.ppermute(mine, "blk", third_of)
        opposite = lax.ppermute(mine, "blk", opposite_of)
        beside = paired(own, next_pairs)
        last = tick + 1 == ticks
        sums = partial_sums(place, kept, given, own, beside, third, opposite, last)
        if last:
            carry = carry_sum(place, sums[1], paired(sums[0], chip_pairs))
        else:
            moved = lax.ppermute(sums, "grp", [(g, g + 1) for g in range(groups - 1)])
            both = paired(moved, chip_pairs)
            solved, own = pair_solve(tick + 1, place, both, right_side, inverse_diag, given)
            solved_ticks.append(solved)
    return (jnp.stack(solved_ticks), carry)


def solution(mesh):
    placed = (
        P(None, ("grp", "blk"), None),
        P(("grp", "blk"), None),
        P(("grp", "blk"), None, None, None),
        P(("grp", "blk"), None),
        P(("grp", "blk")),
        P(("grp", "blk"), None),
    )
    return jax.shard_map(
        shards,
        mesh=mesh,
        in_specs=placed,
        out_specs=(P(None, ("grp", "blk"), None), P(("grp", "blk"), None)),
        check_vma=False,
    )
```

```python
import functools

import jax
import jax.numpy as jnp
from jax import lax
from jax.experimental import pallas as pl
from jax.experimental.pallas import tpu as pltpu
from jax.sharding import PartitionSpec as P

F32 = jnp.float32
BF16 = jnp.bfloat16
VMEM = pl.BlockSpec(memory_space=pltpu.VMEM)
SMEM = pl.BlockSpec(memory_space=pltpu.SMEM)
HBM = pl.BlockSpec(memory_space=pltpu.HBM)
LIMIT = 20 * 1024 * 1024


def params():
    return pltpu.CompilerParams(vmem_limit_bytes=LIMIT)


def mm(a, b):
    return jnp.dot(a, b, preferred_element_type=F32)


def combine_kernel(around, source_list, count, blocks, inverse, right, kept, handed, landing, sums, arrived):
    block = inverse.shape[0]
    live = count[0]
    own = lax.axis_index("blk")
    sign = 2 * lax.rem(own, 2) - 1

    def copy_of(k):
        return pltpu.make_async_copy(blocks.at[0, k], landing.at[k], arrived.at[k])

    def begin(k, carry):
        copy_of(k).start()
        return carry

    lax.fori_loop(0, live, begin, 0)
    sums[...] = jnp.zeros_like(sums)
    handed[3 * block : 4 * block, :] = inverse[...]
    for tick in range(1, right.shape[0]):
        value = right[tick]
        high = value.astype(BF16)
        rows = pl.ds((3 + tick) * block, block)
        handed[rows, 0 : value.shape[1]] = high
        handed[rows, value.shape[1] :] = (value - high.astype(F32)).astype(BF16)

    def add(k, carry):
        copy_of(k).wait()
        offset = lax.rem(source_list[0, k] - own + 3 + around, around) - 3
        turned = offset * sign
        slot = jnp.where(k == 0, 4, jnp.where(turned >= 0, 3 - turned, 8 + turned))
        sums[slot] = sums[slot] + landing[k].astype(F32)
        return carry

    lax.fori_loop(0, live, add, 0)
    for i in range(5):
        kept[i] = sums[i].astype(BF16)
    for i in range(3):
        handed[i * block : (i + 1) * block, :] = sums[5 + i].astype(BF16)


def combine(around, sources, counts, factor_blocks, inverse_diag, right_side):
    slots, block = factor_blocks.shape[1], factor_blocks.shape[2]
    ticks = right_side.shape[0]
    return pl.pallas_call(
        functools.partial(combine_kernel, around),
        out_shape=(
            jax.ShapeDtypeStruct((5, block, block), BF16),
            jax.ShapeDtypeStruct(((3 + ticks) * block, block), BF16),
        ),
        in_specs=[SMEM, SMEM, HBM, VMEM, VMEM],
        out_specs=(VMEM, VMEM),
        scratch_shapes=[
            pltpu.VMEM((slots, block, block), BF16),
            pltpu.VMEM((8, block, block), F32),
            pltpu.SemaphoreType.DMA((slots,)),
        ],
        compiler_params=params(),
        cost_estimate=pl.CostEstimate(flops=4_000_000, bytes_accessed=10_000_000, transcendentals=0),
        name="combine",
    )(sources, counts, factor_blocks, inverse_diag, right_side)


def first_kernel(right, incoming, inverse, solved, outgoing, right_here, incoming_here, inverse_here, arrived):
    copies = (
        pltpu.make_async_copy(right.at[0], right_here, arrived.at[0]),
        pltpu.make_async_copy(incoming, incoming_here, arrived.at[1]),
        pltpu.make_async_copy(inverse, inverse_here, arrived.at[2]),
    )
    for copy in copies:
        copy.start()
    for copy in copies:
        copy.wait()
    value = mm(inverse_here[...], (right_here[...] - incoming_here[...]).astype(BF16))
    solved[...] = value
    outgoing[...] = value.astype(BF16)


def first_solve(right_side, carry_in, inverse_diag):
    ticks, block, columns = right_side.shape
    return pl.pallas_call(
        first_kernel,
        out_shape=(
            jax.ShapeDtypeStruct((block, columns), F32),
            jax.ShapeDtypeStruct((block, columns), BF16),
        ),
        in_specs=[HBM, HBM, HBM],
        out_specs=(VMEM, VMEM),
        scratch_shapes=[
            pltpu.VMEM((block, columns), F32),
            pltpu.VMEM((block, columns), F32),
            pltpu.VMEM((block, block), BF16),
            pltpu.SemaphoreType.DMA((3,)),
        ],
        compiler_params=params(),
        name="first",
    )(right_side, carry_in, inverse_diag)


def pair_kernel(tick, both, right, inverse, given, solved, outgoing):
    block, columns = solved.shape
    odd = lax.rem(lax.axis_index("blk"), 2)
    mine = odd * (2 * block)
    theirs = (1 - odd) * (2 * block)

    def part(at):
        return both[pl.ds(pl.multiple_of(at, block), block), :].astype(F32)

    incoming = part(mine) + part(theirs + block)
    other = part(mine + block) + part(theirs)
    value = mm(inverse[...], (right[tick] - incoming).astype(BF16))
    solved[...] = value
    outgoing[0:block] = value.astype(BF16)
    rows = pl.ds((3 + tick) * block, block)
    other_right = given[rows, 0:columns].astype(F32) + given[rows, columns:].astype(F32)
    value = mm(given[3 * block : 4 * block, :], (other_right - other).astype(BF16))
    outgoing[block:] = value.astype(BF16)


def pair_solve(tick, both, right_side, inverse_diag, given):
    ticks, block, columns = right_side.shape
    return pl.pallas_call(
        functools.partial(pair_kernel, tick),
        out_shape=(
            jax.ShapeDtypeStruct((block, columns), F32),
            jax.ShapeDtypeStruct((2 * block, columns), BF16),
        ),
        in_specs=[VMEM, VMEM, VMEM, VMEM],
        out_specs=(VMEM, VMEM),
        compiler_params=params(),
        name="solve",
    )(both, right_side, inverse_diag, given)


def partial_kernel(tick, last, kept, given, own, beside, third, opposite, solved, *refs):
    sums, outputs, leaving = refs[-3:]
    copy = pltpu.make_async_copy(solved, outputs.at[tick], leaving)
    copy.start()
    block = own.shape[0] // 2
    near = lax.rem(lax.axis_index("blk"), 2) * (2 * block)

    def part(at):
        return beside[pl.ds(pl.multiple_of(at, block), block), :]

    odd_one, same_one = part(near), part(near + block)
    self_one = own[0:block]
    value = mm(kept[3], self_one)
    value += mm(kept[1], same_one)
    value += mm(kept[2], odd_one)
    value += mm(kept[0], third[...])
    value += mm(kept[4], opposite[...])
    other = mm(given[0:block, :], same_one)
    other += mm(given[block : 2 * block, :], odd_one)
    other += mm(given[2 * block : 3 * block, :], self_one)
    if last:
        refs[-4][...] = value
        sums[...] = other.astype(BF16)
    else:
        sums[0:block] = value.astype(BF16)
        sums[block:] = other.astype(BF16)
    copy.wait()


def partial_sums(tick, ticks, kept, given, own, beside, third, opposite, solved, outputs):
    block, columns = third.shape
    last = tick + 1 == ticks
    shapes = [jax.ShapeDtypeStruct((ticks, block, columns), F32)]
    specs = [VMEM, HBM]
    if last:
        shapes = [
            jax.ShapeDtypeStruct((block, columns), F32),
            jax.ShapeDtypeStruct((block, columns), BF16),
        ] + shapes
        specs = [VMEM] + specs
    else:
        shapes = [jax.ShapeDtypeStruct((2 * block, columns), BF16)] + shapes
    operands = [kept, given, own, beside, third, opposite, solved]
    in_specs = [VMEM] * 7
    aliases = {}
    if outputs is not None:
        aliases = {len(operands): len(shapes) - 1}
        operands.append(outputs)
        in_specs.append(HBM)
    return pl.pallas_call(
        functools.partial(partial_kernel, tick, last),
        out_shape=tuple(shapes),
        in_specs=in_specs,
        out_specs=tuple(specs),
        input_output_aliases=aliases,
        scratch_shapes=[pltpu.SemaphoreType.DMA],
        compiler_params=params(),
        name="partial",
    )(*operands)


def carry_kernel(exact, both, carry):
    block = exact.shape[0]
    odd = lax.rem(lax.axis_index("blk"), 2)
    theirs = pl.multiple_of((1 - odd) * block, block)
    carry[...] = exact[...] + both[pl.ds(theirs, block), :].astype(F32)


def carry_sum(exact, both):
    return pl.pallas_call(
        carry_kernel,
        out_shape=jax.ShapeDtypeStruct(exact.shape, F32),
        in_specs=[VMEM, VMEM],
        out_specs=VMEM,
        compiler_params=params(),
        name="carry",
    )(exact, both)


def shards(right_side, inverse_diag, factor_blocks, sources, counts, carry_in):
    ticks, block = right_side.shape[0], right_side.shape[1]
    groups, around = lax.axis_size("grp"), lax.axis_size("blk")
    chips = around // 2
    at = lax.axis_index("blk").astype(jnp.int32)
    odd = lax.rem(at, 2)
    chip_pairs = [[2 * c, 2 * c + 1] for c in range(chips)]
    next_pairs = [[2 * c + 1, (2 * c + 2) % around] for c in range(chips)]
    third_pairs = [[2 * c + 1, (2 * c + 4) % around] for c in range(chips)]
    opposite_pairs = [[b, b + chips] for b in range(chips)]

    def paired(value, pairs):
        return lax.all_gather(value, "blk", axis=0, tiled=True, axis_index_groups=pairs)

    def swapped(value, pairs):
        partner = [(a, b) for a, b in pairs] + [(b, a) for a, b in pairs]
        return lax.ppermute(value, "blk", partner)

    solved, own = first_solve(right_side, carry_in, inverse_diag)
    outputs = kept = given = None
    for tick in range(ticks):
        mine = own[0:block]
        third = swapped(mine, third_pairs)
        opposite = swapped(mine, opposite_pairs)
        if tick == 0:
            chip = paired(own, chip_pairs)
            own = jnp.where(odd == 0, chip, jnp.roll(chip, block, 0))
            near = swapped(own, next_pairs)
            beside = jnp.concatenate([near, near], 0)
            held = (sources, counts, factor_blocks, inverse_diag, right_side)
            held = lax.optimization_barrier((own, *held))[1:]
            kept, handed = combine(around, *held)
            given = swapped(handed, chip_pairs)
        else:
            beside = paired(own, next_pairs)
        *sums, outputs = partial_sums(tick, ticks, kept, given, own, beside, third, opposite, solved, outputs)
        if tick + 1 == ticks:
            carry = carry_sum(sums[0], paired(sums[1], chip_pairs))
        else:
            moved = lax.ppermute(sums[0], "grp", [(g, g + 1) for g in range(groups - 1)])
            both = paired(moved, chip_pairs)
            solved, own = pair_solve(tick + 1, both, right_side, inverse_diag, given)
    return (outputs, carry)


def solution(mesh):
    placed = (
        P(None, ("grp", "blk"), None),
        P(("grp", "blk"), None),
        P(("grp", "blk"), None, None, None),
        P(("grp", "blk"), None),
        P(("grp", "blk")),
        P(("grp", "blk"), None),
    )
    return jax.shard_map(
        shards,
        mesh=mesh,
        in_specs=placed,
        out_specs=(P(None, ("grp", "blk"), None), P(("grp", "blk"), None)),
        check_vma=False,
    )
```

```python
import functools

import jax
import jax.numpy as jnp
from jax import lax
from jax.experimental import pallas as pl
from jax.experimental.pallas import tpu as pltpu
from jax.sharding import PartitionSpec as P

F32 = jnp.float32
BF16 = jnp.bfloat16
VMEM = pl.BlockSpec(memory_space=pltpu.VMEM)
HBM = pl.BlockSpec(memory_space=pltpu.HBM)
LIMIT = 20 * 1024 * 1024


def params():
    return pltpu.CompilerParams(vmem_limit_bytes=LIMIT)


def mm(a, b):
    return jnp.dot(a, b, preferred_element_type=F32)


def combine_kernel(around, listed, blocks, inverse, right, kept, handed, listed_here, landing, sums, arrived, small):
    block = inverse.shape[0]
    copy = pltpu.make_async_copy(listed, listed_here, small)
    copy.start()
    own = lax.axis_index("blk")
    sign = 2 * lax.rem(own, 2) - 1

    def copy_of(k):
        return pltpu.make_async_copy(blocks.at[0, k], landing.at[k], arrived.at[k])

    copy.wait()
    live = listed_here[0, blocks.shape[1]]

    def begin(k, carry):
        copy_of(k).start()
        return carry

    lax.fori_loop(0, live, begin, 0)
    sums[...] = jnp.zeros_like(sums)
    handed[4 * block : 5 * block, :] = inverse[...]
    for tick in range(right.shape[0]):
        value = right[tick]
        high = value.astype(BF16)
        rows = pl.ds((5 + tick) * block, block)
        handed[rows, 0 : value.shape[1]] = high
        handed[rows, value.shape[1] :] = (value - high.astype(F32)).astype(BF16)

    def add(k, carry):
        copy_of(k).wait()
        offset = lax.rem(listed_here[0, k] - own + 3 + around, around) - 3
        turned = offset * sign
        slot = jnp.where(k == 0, 4, jnp.where(turned >= 0, 3 - turned, 8 + turned))
        sums[slot] = sums[slot] + landing[k].astype(F32)
        return carry

    lax.fori_loop(0, live, add, 0)
    for i in range(5):
        kept[i] = sums[i].astype(BF16)
    for i in range(3):
        handed[i * block : (i + 1) * block, :] = sums[5 + i].astype(BF16)
    handed[3 * block : 4 * block, :] = sums[4].astype(BF16)


def in_hbm(value):
    return pltpu.with_memory_space_constraint(value, pltpu.HBM)


def combine(around, sources, counts, factor_blocks, inverse, right):
    slots, block = factor_blocks.shape[1], factor_blocks.shape[2]
    ticks = right.shape[0]
    listed = jnp.concatenate([sources, counts[:, None]], 1)
    return pl.pallas_call(
        functools.partial(combine_kernel, around),
        out_shape=(
            jax.ShapeDtypeStruct((5, block, block), BF16),
            jax.ShapeDtypeStruct(((5 + ticks) * block, block), BF16),
        ),
        in_specs=[HBM, HBM, VMEM, VMEM],
        out_specs=(VMEM, VMEM),
        scratch_shapes=[
            pltpu.SMEM(listed.shape, jnp.int32),
            pltpu.VMEM((slots, block, block), BF16),
            pltpu.VMEM((8, block, block), F32),
            pltpu.SemaphoreType.DMA((slots,)),
            pltpu.SemaphoreType.DMA,
        ],
        compiler_params=params(),
        cost_estimate=pl.CostEstimate(flops=4_000_000, bytes_accessed=10_000_000, transcendentals=0),
        name="combine",
    )(in_hbm(listed), in_hbm(factor_blocks), inverse, right)


def first_kernel(right, incoming, inverse, solved, outgoing, inverse_here, later_here, right_here, incoming_here, arrived):
    copies = (
        pltpu.make_async_copy(right.at[0], right_here, arrived.at[0]),
        pltpu.make_async_copy(incoming, incoming_here, arrived.at[1]),
        pltpu.make_async_copy(inverse, inverse_here, arrived.at[2]),
        pltpu.make_async_copy(right.at[pl.ds(1, later_here.shape[0])], later_here, arrived.at[3]),
    )
    for copy in copies:
        copy.start()
    for copy in copies[:3]:
        copy.wait()
    value = mm(inverse_here[...], (right_here[...] - incoming_here[...]).astype(BF16))
    solved[...] = value
    outgoing[...] = value.astype(BF16)
    copies[3].wait()


def first_solve(right_side, carry_in, inverse_diag):
    ticks, block, columns = right_side.shape
    return pl.pallas_call(
        first_kernel,
        out_shape=(
            jax.ShapeDtypeStruct((block, columns), F32),
            jax.ShapeDtypeStruct((block, columns), BF16),
            jax.ShapeDtypeStruct((block, block), BF16),
            jax.ShapeDtypeStruct((ticks - 1, block, columns), F32),
        ),
        in_specs=[HBM, HBM, HBM],
        out_specs=(VMEM, VMEM, VMEM, VMEM),
        scratch_shapes=[
            pltpu.VMEM((block, columns), F32),
            pltpu.VMEM((block, columns), F32),
            pltpu.SemaphoreType.DMA((4,)),
        ],
        compiler_params=params(),
        name="first",
    )(in_hbm(right_side), in_hbm(carry_in), in_hbm(inverse_diag))


def pair_kernel(tick, both, right, inverse, given, *refs):
    far = refs[:-2]
    solved, outgoing = refs[-2:]
    block, columns = solved.shape
    odd = lax.rem(lax.axis_index("blk"), 2)
    mine = odd * (2 * block)
    theirs = (1 - odd) * (2 * block)

    def part(at):
        return both[pl.ds(pl.multiple_of(at, block), block), :].astype(F32)

    incoming = part(mine) + part(theirs + block)
    other = part(mine + block) + part(theirs)
    for ref in far:
        incoming += ref[0:block].astype(F32)
        other += ref[block:].astype(F32)
    value = mm(inverse[...], (right[tick - 1] - incoming).astype(BF16))
    solved[...] = value
    outgoing[0:block] = value.astype(BF16)
    rows = pl.ds((4 + tick) * block, block)
    other_right = given[rows, 0:columns].astype(F32) + given[rows, columns:].astype(F32)
    value = mm(given[4 * block : 5 * block, :], (other_right - other).astype(BF16))
    outgoing[block:] = value.astype(BF16)


def pair_solve(tick, both, right, inverse, given, far):
    block, columns = right.shape[1:]
    operands = [both, right, inverse, given] + ([] if far is None else [far])
    return pl.pallas_call(
        functools.partial(pair_kernel, tick),
        out_shape=(
            jax.ShapeDtypeStruct((block, columns), F32),
            jax.ShapeDtypeStruct((2 * block, columns), BF16),
        ),
        in_specs=[VMEM] * len(operands),
        out_specs=(VMEM, VMEM),
        compiler_params=params(),
        name="solve",
    )(*operands)


def products(kept, given, own, beside, third, opposite):
    block = third.shape[0]
    near = lax.rem(lax.axis_index("blk"), 2) * (2 * block)

    def part(at):
        return beside[pl.ds(pl.multiple_of(at, block), block), :]

    odd_one, same_one = part(near), part(near + block)
    self_one = own[0:block]
    value = mm(kept[3], self_one)
    value += mm(kept[1], same_one)
    value += mm(kept[2], odd_one)
    value += mm(kept[0], third[...])
    if opposite is not None:
        value += mm(kept[4], opposite[...])
    other = mm(given[0:block, :], same_one)
    other += mm(given[block : 2 * block, :], odd_one)
    other += mm(given[2 * block : 3 * block, :], self_one)
    return value, other


def partial_kernel(kept, given, own, beside, third, opposite, sums):
    block = third.shape[0]
    value, other = products(kept, given, own, beside, third, opposite)
    sums[0:block] = value.astype(BF16)
    sums[block:] = other.astype(BF16)


def far_kernel(kept, given, own, beside, third, far_sums, sums, leaving):
    block = third.shape[0]
    value, other = products(kept, given, own, beside, third, None)
    sums[0:block] = value.astype(BF16)
    sums[block:] = other.astype(BF16)
    leaving[0:block] = mm(far_sums[0:block, :], own[0:block]).astype(BF16)
    leaving[block:] = mm(far_sums[block:, :], own[block:]).astype(BF16)


def last_kernel(ticks, kept, given, own, beside, third, opposite, *refs):
    solved = refs[:ticks]
    exact, sums, outputs, left = refs[ticks:]
    copies = [pltpu.make_async_copy(solved[t], outputs.at[t], left.at[t]) for t in range(ticks)]
    for copy in copies:
        copy.start()
    value, other = products(kept, given, own, beside, third, opposite)
    exact[...] = value
    sums[...] = other.astype(BF16)
    for copy in copies:
        copy.wait()


def partial_sums(kernel, operands, pairs_out):
    block, columns = operands[4].shape
    return pl.pallas_call(
        kernel,
        out_shape=(jax.ShapeDtypeStruct((2 * block, columns), BF16),) * pairs_out,
        in_specs=[VMEM] * len(operands),
        out_specs=(VMEM,) * pairs_out,
        compiler_params=params(),
        name="partial",
    )(*operands)


def last_sums(operands, solved):
    block, columns = operands[4].shape
    ticks = len(solved)
    return pl.pallas_call(
        functools.partial(last_kernel, ticks),
        out_shape=(
            jax.ShapeDtypeStruct((block, columns), F32),
            jax.ShapeDtypeStruct((block, columns), BF16),
            jax.ShapeDtypeStruct((ticks, block, columns), F32),
        ),
        in_specs=[VMEM] * (len(operands) + ticks),
        out_specs=(VMEM, VMEM, HBM),
        scratch_shapes=[pltpu.SemaphoreType.DMA((ticks,))],
        compiler_params=params(),
        name="last",
    )(*operands, *solved)


def carry_kernel(exact, both, carry):
    block = exact.shape[0]
    odd = lax.rem(lax.axis_index("blk"), 2)
    theirs = pl.multiple_of((1 - odd) * block, block)
    carry[...] = exact[...] + both[pl.ds(theirs, block), :].astype(F32)


def carry_sum(exact, both):
    return pl.pallas_call(
        carry_kernel,
        out_shape=jax.ShapeDtypeStruct(exact.shape, F32),
        in_specs=[VMEM, VMEM],
        out_specs=VMEM,
        compiler_params=params(),
        name="carry",
    )(exact, both)


def shards(right_side, inverse_diag, factor_blocks, sources, counts, carry_in):
    ticks, block = right_side.shape[0], right_side.shape[1]
    groups, around = lax.axis_size("grp"), lax.axis_size("blk")
    chips = around // 2
    at = lax.axis_index("blk").astype(jnp.int32)
    odd = lax.rem(at, 2)
    chip_pairs = [[2 * c, 2 * c + 1] for c in range(chips)]
    next_pairs = [[2 * c + 1, (2 * c + 2) % around] for c in range(chips)]
    third_pairs = [[2 * c + 1, (2 * c + 4) % around] for c in range(chips)]
    opposite_pairs = [[b, b + chips] for b in range(chips)]

    def paired(value, pairs):
        return lax.all_gather(value, "blk", axis=0, tiled=True, axis_index_groups=pairs)

    def swapped(value, pairs):
        partner = [(a, b) for a, b in pairs] + [(b, a) for a, b in pairs]
        return lax.ppermute(value, "blk", partner)

    solved, own, inverse, right = first_solve(right_side, carry_in, inverse_diag)
    finished = [solved]
    far_sums = None
    forward = [(g * around + (b + chips) % around, (g + 1) * around + b) for g in range(groups - 1) for b in range(around)]
    for tick in range(ticks):
        last = tick + 1 == ticks
        near_form = tick == 0 or last
        mine = own[0:block]
        third = swapped(mine, third_pairs)
        opposite = swapped(mine, opposite_pairs) if near_form else None
        if tick == 0:
            chip = paired(own, chip_pairs)
            own = jnp.where(odd == 0, chip, jnp.roll(chip, block, 0))
            near = swapped(own, next_pairs)
            held = (own, third, opposite, sources, counts, factor_blocks, inverse, right)
            own, third, opposite, *held = lax.optimization_barrier(held)
            kept, handed = combine(around, *held)
            near, handed = lax.optimization_barrier((near, handed))
            given = swapped(handed, chip_pairs)
            beside = jnp.concatenate([near, near], 0)
        else:
            beside = paired(own, next_pairs)
        operands = [kept, given, own, beside, third]
        if last:
            exact, crossing, outputs = last_sums(operands + [opposite], finished)
            carry = carry_sum(exact, paired(crossing, chip_pairs))
            return (outputs, carry)
        far = None
        if near_form:
            (sums,) = partial_sums(partial_kernel, operands + [opposite], 1)
            own_far, pair_far = lax.optimization_barrier((sums, kept[4], given[3 * block : 4 * block]))[1:]
            far_sums = swapped(jnp.concatenate([own_far, pair_far], 0), opposite_pairs)
        else:
            sums, leaving = partial_sums(far_kernel, operands + [far_sums], 2)
            far = lax.ppermute(leaving, ("grp", "blk"), forward)
        moved = lax.ppermute(sums, "grp", [(g, g + 1) for g in range(groups - 1)])
        both = paired(moved, chip_pairs)
        solved, own = pair_solve(tick + 1, both, right, inverse, given, far)
        finished.append(solved)


def solution(mesh):
    placed = (
        P(None, ("grp", "blk"), None),
        P(("grp", "blk"), None),
        P(("grp", "blk"), None, None, None),
        P(("grp", "blk"), None),
        P(("grp", "blk")),
        P(("grp", "blk"), None),
    )
    return jax.shard_map(
        shards,
        mesh=mesh,
        in_specs=placed,
        out_specs=(P(None, ("grp", "blk"), None), P(("grp", "blk"), None)),
        check_vma=False,
    )
```

```python
import functools

import jax
import jax.numpy as jnp
from jax import lax
from jax.experimental import pallas as pl
from jax.experimental.pallas import tpu as pltpu
from jax.sharding import PartitionSpec as P

F32 = jnp.float32
BF16 = jnp.bfloat16
VMEM = pl.BlockSpec(memory_space=pltpu.VMEM)
SMEM = pl.BlockSpec(memory_space=pltpu.SMEM)
HBM = pl.BlockSpec(memory_space=pltpu.HBM)
LIMIT = 20 * 1024 * 1024


def params():
    return pltpu.CompilerParams(vmem_limit_bytes=LIMIT)


def mm(a, b):
    return jnp.dot(a, b, preferred_element_type=F32)


def combine_kernel(around, count, source_list, blocks, inverse, right, kept, handed, source_here, landing, sums, arrived, small):
    block = inverse.shape[0]
    copy = pltpu.make_async_copy(source_list, source_here, small)
    copy.start()
    own = lax.axis_index("blk")
    sign = 2 * lax.rem(own, 2) - 1

    def copy_of(k):
        return pltpu.make_async_copy(blocks.at[0, k], landing.at[k], arrived.at[k])

    live = count[0]

    def begin(k, carry):
        copy_of(k).start()
        return carry

    lax.fori_loop(0, live, begin, 0)
    sums[...] = jnp.zeros_like(sums)
    handed[4 * block : 5 * block, :] = inverse[...]
    for tick in range(right.shape[0]):
        value = right[tick]
        high = value.astype(BF16)
        rows = pl.ds((5 + tick) * block, block)
        handed[rows, 0 : value.shape[1]] = high
        handed[rows, value.shape[1] :] = (value - high.astype(F32)).astype(BF16)
    copy.wait()

    def add(k, carry):
        copy_of(k).wait()
        offset = lax.rem(source_here[0, k] - own + 3 + around, around) - 3
        turned = offset * sign
        slot = jnp.where(k == 0, 4, jnp.where(turned >= 0, 3 - turned, 8 + turned))
        sums[slot] = sums[slot] + landing[k].astype(F32)
        return carry

    lax.fori_loop(0, live, add, 0)
    for i in range(5):
        kept[i] = sums[i].astype(BF16)
    for i in range(3):
        handed[i * block : (i + 1) * block, :] = sums[5 + i].astype(BF16)
    handed[3 * block : 4 * block, :] = sums[4].astype(BF16)


def in_hbm(value):
    return pltpu.with_memory_space_constraint(value, pltpu.HBM)


def combine(around, sources, counts, factor_blocks, inverse, right):
    slots, block = factor_blocks.shape[1], factor_blocks.shape[2]
    ticks = right.shape[0]
    return pl.pallas_call(
        functools.partial(combine_kernel, around),
        out_shape=(
            jax.ShapeDtypeStruct((5, block, block), BF16),
            jax.ShapeDtypeStruct(((5 + ticks) * block, block), BF16),
        ),
        in_specs=[SMEM, HBM, HBM, VMEM, VMEM],
        out_specs=(VMEM, VMEM),
        scratch_shapes=[
            pltpu.SMEM(sources.shape, jnp.int32),
            pltpu.VMEM((slots, block, block), BF16),
            pltpu.VMEM((8, block, block), F32),
            pltpu.SemaphoreType.DMA((slots,)),
            pltpu.SemaphoreType.DMA,
        ],
        compiler_params=params(),
        cost_estimate=pl.CostEstimate(flops=4_000_000, bytes_accessed=10_000_000, transcendentals=0),
        name="combine",
    )(counts, in_hbm(sources), in_hbm(factor_blocks), inverse, right)


def first_kernel(right, incoming, inverse, solved, outgoing, inverse_here, later_here, right_here, incoming_here, arrived):
    copies = (
        pltpu.make_async_copy(right.at[0], right_here, arrived.at[0]),
        pltpu.make_async_copy(incoming, incoming_here, arrived.at[1]),
        pltpu.make_async_copy(inverse, inverse_here, arrived.at[2]),
        pltpu.make_async_copy(right.at[pl.ds(1, later_here.shape[0])], later_here, arrived.at[3]),
    )
    for copy in copies:
        copy.start()
    for copy in copies[:3]:
        copy.wait()
    value = mm(inverse_here[...], (right_here[...] - incoming_here[...]).astype(BF16))
    solved[...] = value
    outgoing[...] = value.astype(BF16)
    copies[3].wait()


def first_solve(right_side, carry_in, inverse_diag):
    ticks, block, columns = right_side.shape
    return pl.pallas_call(
        first_kernel,
        out_shape=(
            jax.ShapeDtypeStruct((block, columns), F32),
            jax.ShapeDtypeStruct((block, columns), BF16),
            jax.ShapeDtypeStruct((block, block), BF16),
            jax.ShapeDtypeStruct((ticks - 1, block, columns), F32),
        ),
        in_specs=[HBM, HBM, HBM],
        out_specs=(VMEM, VMEM, VMEM, VMEM),
        scratch_shapes=[
            pltpu.VMEM((block, columns), F32),
            pltpu.VMEM((block, columns), F32),
            pltpu.SemaphoreType.DMA((4,)),
        ],
        compiler_params=params(),
        name="first",
    )(in_hbm(right_side), in_hbm(carry_in), in_hbm(inverse_diag))


def pair_kernel(tick, both, right, inverse, given, *refs):
    far = refs[:-2]
    solved, outgoing = refs[-2:]
    block, columns = solved.shape
    odd = lax.rem(lax.axis_index("blk"), 2)
    mine = odd * (2 * block)
    theirs = (1 - odd) * (2 * block)

    def part(at):
        return both[pl.ds(pl.multiple_of(at, block), block), :].astype(F32)

    incoming = part(mine) + part(theirs + block)
    other = part(mine + block) + part(theirs)
    for ref in far:
        incoming += ref[0:block].astype(F32)
        other += ref[block:].astype(F32)
    value = mm(inverse[...], (right[tick - 1] - incoming).astype(BF16))
    solved[...] = value
    outgoing[0:block] = value.astype(BF16)
    rows = pl.ds((4 + tick) * block, block)
    other_right = given[rows, 0:columns].astype(F32) + given[rows, columns:].astype(F32)
    value = mm(given[4 * block : 5 * block, :], (other_right - other).astype(BF16))
    outgoing[block:] = value.astype(BF16)


def pair_solve(tick, both, right, inverse, given, far):
    block, columns = right.shape[1:]
    operands = [both, right, inverse, given] + ([] if far is None else [far])
    return pl.pallas_call(
        functools.partial(pair_kernel, tick),
        out_shape=(
            jax.ShapeDtypeStruct((block, columns), F32),
            jax.ShapeDtypeStruct((2 * block, columns), BF16),
        ),
        in_specs=[VMEM] * len(operands),
        out_specs=(VMEM, VMEM),
        compiler_params=params(),
        name="solve",
    )(*operands)


def products(kept, given, own, beside, third, opposite):
    block = third.shape[0]
    odd_one, same_one = beside[0:block], beside[block:]
    self_one = own[0:block]
    value = mm(kept[3], self_one)
    value += mm(kept[1], same_one)
    value += mm(kept[2], odd_one)
    value += mm(kept[0], third[...])
    if opposite is not None:
        value += mm(kept[4], opposite[...])
    other = mm(given[0:block, :], same_one)
    other += mm(given[block : 2 * block, :], odd_one)
    other += mm(given[2 * block : 3 * block, :], self_one)
    return value, other


def partial_kernel(kept, given, own, beside, third, opposite, sums):
    block = third.shape[0]
    value, other = products(kept, given, own, beside, third, opposite)
    sums[0:block] = value.astype(BF16)
    sums[block:] = other.astype(BF16)


def far_kernel(kept, given, own, beside, third, far_sums, sums, leaving):
    block = third.shape[0]
    value, other = products(kept, given, own, beside, third, None)
    sums[0:block] = value.astype(BF16)
    sums[block:] = other.astype(BF16)
    leaving[0:block] = mm(far_sums[0:block, :], own[0:block]).astype(BF16)
    leaving[block:] = mm(far_sums[block:, :], own[block:]).astype(BF16)


def last_kernel(ticks, kept, given, own, beside, third, opposite, *refs):
    solved = refs[:ticks]
    exact, sums, outputs, left = refs[ticks:]
    copies = [pltpu.make_async_copy(solved[t], outputs.at[t], left.at[t]) for t in range(ticks)]
    for copy in copies:
        copy.start()
    value, other = products(kept, given, own, beside, third, opposite)
    exact[...] = value
    sums[...] = other.astype(BF16)
    for copy in copies:
        copy.wait()


def partial_sums(kernel, operands, pairs_out):
    block, columns = operands[4].shape
    return pl.pallas_call(
        kernel,
        out_shape=(jax.ShapeDtypeStruct((2 * block, columns), BF16),) * pairs_out,
        in_specs=[VMEM] * len(operands),
        out_specs=(VMEM,) * pairs_out,
        compiler_params=params(),
        name="partial",
    )(*operands)


def last_sums(operands, solved):
    block, columns = operands[4].shape
    ticks = len(solved)
    return pl.pallas_call(
        functools.partial(last_kernel, ticks),
        out_shape=(
            jax.ShapeDtypeStruct((block, columns), F32),
            jax.ShapeDtypeStruct((block, columns), BF16),
            jax.ShapeDtypeStruct((ticks, block, columns), F32),
        ),
        in_specs=[VMEM] * (len(operands) + ticks),
        out_specs=(VMEM, VMEM, HBM),
        scratch_shapes=[pltpu.SemaphoreType.DMA((ticks,))],
        compiler_params=params(),
        name="last",
    )(*operands, *solved)


def carry_kernel(exact, both, carry):
    block = exact.shape[0]
    odd = lax.rem(lax.axis_index("blk"), 2)
    theirs = pl.multiple_of((1 - odd) * block, block)
    carry[...] = exact[...] + both[pl.ds(theirs, block), :].astype(F32)


def carry_sum(exact, both):
    return pl.pallas_call(
        carry_kernel,
        out_shape=jax.ShapeDtypeStruct(exact.shape, F32),
        in_specs=[VMEM, VMEM],
        out_specs=VMEM,
        compiler_params=params(),
        name="carry",
    )(exact, both)


def shards(right_side, inverse_diag, factor_blocks, sources, counts, carry_in):
    ticks, block = right_side.shape[0], right_side.shape[1]
    groups, around = lax.axis_size("grp"), lax.axis_size("blk")
    chips = around // 2
    at = lax.axis_index("blk").astype(jnp.int32)
    odd = lax.rem(at, 2)
    chip_pairs = [[2 * c, 2 * c + 1] for c in range(chips)]
    next_pairs = [[2 * c + 1, (2 * c + 2) % around] for c in range(chips)]
    third_pairs = [[2 * c + 1, (2 * c + 4) % around] for c in range(chips)]
    opposite_pairs = [[b, b + chips] for b in range(chips)]

    def paired(value, pairs):
        return lax.all_gather(value, "blk", axis=0, tiled=True, axis_index_groups=pairs)

    def swapped(value, pairs):
        partner = [(a, b) for a, b in pairs] + [(b, a) for a, b in pairs]
        return lax.ppermute(value, "blk", partner)

    solved, own, inverse, right = first_solve(right_side, carry_in, inverse_diag)
    finished = [solved]
    far_sums = None
    forward = [(g * around + (b + chips) % around, (g + 1) * around + b) for g in range(groups - 1) for b in range(around)]
    for tick in range(ticks):
        last = tick + 1 == ticks
        near_form = tick == 0 or last
        mine = own[0:block]
        third = swapped(mine, third_pairs)
        opposite = swapped(mine, opposite_pairs) if near_form else None
        if tick == 0:
            chip = paired(own, chip_pairs)
            own = jnp.where(odd == 0, chip, jnp.roll(chip, block, 0))
            beside = swapped(own, next_pairs)
            held = (own, third, opposite, sources, counts, factor_blocks, inverse, right)
            own, third, opposite, *held = lax.optimization_barrier(held)
            kept, handed = combine(around, *held)
            beside, handed = lax.optimization_barrier((beside, handed))
            given = swapped(handed, chip_pairs)
        else:
            beside = swapped(own, next_pairs)
        operands = [kept, given, own, beside, third]
        if last:
            exact, crossing, outputs = last_sums(operands + [opposite], finished)
            carry = carry_sum(exact, paired(crossing, chip_pairs))
            return (outputs, carry)
        far = None
        if near_form:
            (sums,) = partial_sums(partial_kernel, operands + [opposite], 1)
            own_far, pair_far = lax.optimization_barrier((sums, kept[4], given[3 * block : 4 * block]))[1:]
            far_sums = swapped(jnp.concatenate([own_far, pair_far], 0), opposite_pairs)
        else:
            sums, leaving = partial_sums(far_kernel, operands + [far_sums], 2)
            far = lax.ppermute(leaving, ("grp", "blk"), forward)
        moved = lax.ppermute(sums, "grp", [(g, g + 1) for g in range(groups - 1)])
        both = paired(moved, chip_pairs)
        solved, own = pair_solve(tick + 1, both, right, inverse, given, far)
        finished.append(solved)


def solution(mesh):
    placed = (
        P(None, ("grp", "blk"), None),
        P(("grp", "blk"), None),
        P(("grp", "blk"), None, None, None),
        P(("grp", "blk"), None),
        P(("grp", "blk")),
        P(("grp", "blk"), None),
    )
    return jax.shard_map(
        shards,
        mesh=mesh,
        in_specs=placed,
        out_specs=(P(None, ("grp", "blk"), None), P(("grp", "blk"), None)),
        check_vma=False,
    )
```

```python
import functools

import jax
import jax.numpy as jnp
from jax import lax
from jax.experimental import pallas as pl
from jax.experimental.pallas import tpu as pltpu
from jax.sharding import PartitionSpec as P

F32 = jnp.float32
BF16 = jnp.bfloat16
VMEM = pl.BlockSpec(memory_space=pltpu.VMEM)
SMEM = pl.BlockSpec(memory_space=pltpu.SMEM)
HBM = pl.BlockSpec(memory_space=pltpu.HBM)
LIMIT = 20 * 1024 * 1024


def params():
    return pltpu.CompilerParams(vmem_limit_bytes=LIMIT)


def mm(a, b):
    return jnp.dot(a, b, preferred_element_type=F32)


def combine_kernel(around, count, source_list, blocks, inverse, right, kept, handed, source_here, landing, sums, arrived, small):
    block = inverse.shape[0]
    copy = pltpu.make_async_copy(source_list, source_here, small)
    copy.start()
    own = lax.axis_index("blk")
    sign = 2 * lax.rem(own, 2) - 1

    def copy_of(k):
        return pltpu.make_async_copy(blocks.at[0, k], landing.at[k], arrived.at[k])

    live = count[0]

    def begin(k, carry):
        copy_of(k).start()
        return carry

    lax.fori_loop(0, live, begin, 0)
    sums[...] = jnp.zeros_like(sums)
    handed[4 * block : 5 * block, :] = inverse[...]
    for tick in range(right.shape[0]):
        value = right[tick]
        high = value.astype(BF16)
        rows = pl.ds((5 + tick) * block, block)
        handed[rows, 0 : value.shape[1]] = high
        handed[rows, value.shape[1] :] = (value - high.astype(F32)).astype(BF16)
    copy.wait()

    def add(k, carry):
        copy_of(k).wait()
        offset = lax.rem(source_here[0, k] - own + 3 + around, around) - 3
        turned = offset * sign
        slot = jnp.where(k == 0, 4, jnp.where(turned >= 0, 3 - turned, 8 + turned))
        sums[slot] = sums[slot] + landing[k].astype(F32)
        return carry

    lax.fori_loop(0, live, add, 0)
    for i in range(5):
        kept[i] = sums[i].astype(BF16)
    for i in range(3):
        handed[i * block : (i + 1) * block, :] = sums[5 + i].astype(BF16)
    odd = lax.rem(own, 2) == 1
    handed[3 * block : 4 * block, :] = jnp.where(odd, sums[3], sums[4]).astype(BF16)


def in_hbm(value):
    return pltpu.with_memory_space_constraint(value, pltpu.HBM)


def combine(around, sources, counts, factor_blocks, inverse, right):
    slots, block = factor_blocks.shape[1], factor_blocks.shape[2]
    ticks = right.shape[0]
    return pl.pallas_call(
        functools.partial(combine_kernel, around),
        out_shape=(
            jax.ShapeDtypeStruct((5, block, block), BF16),
            jax.ShapeDtypeStruct(((5 + ticks) * block, block), BF16),
        ),
        in_specs=[SMEM, HBM, HBM, VMEM, VMEM],
        out_specs=(VMEM, VMEM),
        scratch_shapes=[
            pltpu.SMEM(sources.shape, jnp.int32),
            pltpu.VMEM((slots, block, block), BF16),
            pltpu.VMEM((8, block, block), F32),
            pltpu.SemaphoreType.DMA((slots,)),
            pltpu.SemaphoreType.DMA,
        ],
        compiler_params=params(),
        cost_estimate=pl.CostEstimate(flops=4_000_000, bytes_accessed=10_000_000, transcendentals=0),
        name="combine",
    )(counts, in_hbm(sources), in_hbm(factor_blocks), inverse, right)


def first_kernel(right, incoming, inverse, solved, outgoing, inverse_here, later_here, right_here, incoming_here, arrived):
    copies = (
        pltpu.make_async_copy(right.at[0], right_here, arrived.at[0]),
        pltpu.make_async_copy(incoming, incoming_here, arrived.at[1]),
        pltpu.make_async_copy(inverse, inverse_here, arrived.at[2]),
        pltpu.make_async_copy(right.at[pl.ds(1, later_here.shape[0])], later_here, arrived.at[3]),
    )
    for copy in copies:
        copy.start()
    for copy in copies[:3]:
        copy.wait()
    value = mm(inverse_here[...], (right_here[...] - incoming_here[...]).astype(BF16))
    solved[...] = value
    outgoing[...] = value.astype(BF16)
    copies[3].wait()


def first_solve(right_side, carry_in, inverse_diag):
    ticks, block, columns = right_side.shape
    return pl.pallas_call(
        first_kernel,
        out_shape=(
            jax.ShapeDtypeStruct((block, columns), F32),
            jax.ShapeDtypeStruct((block, columns), BF16),
            jax.ShapeDtypeStruct((block, block), BF16),
            jax.ShapeDtypeStruct((ticks - 1, block, columns), F32),
        ),
        in_specs=[HBM, HBM, HBM],
        out_specs=(VMEM, VMEM, VMEM, VMEM),
        scratch_shapes=[
            pltpu.VMEM((block, columns), F32),
            pltpu.VMEM((block, columns), F32),
            pltpu.SemaphoreType.DMA((4,)),
        ],
        compiler_params=params(),
        name="first",
    )(in_hbm(right_side), in_hbm(carry_in), in_hbm(inverse_diag))


def pair_kernel(tick, both, right, inverse, given, solved, outgoing):
    block, columns = solved.shape
    odd = lax.rem(lax.axis_index("blk"), 2)
    mine = odd * (2 * block)
    theirs = (1 - odd) * (2 * block)

    def part(at):
        return both[pl.ds(pl.multiple_of(at, block), block), :].astype(F32)

    incoming = part(mine) + part(theirs + block)
    other = part(mine + block) + part(theirs)
    value = mm(inverse[...], (right[tick - 1] - incoming).astype(BF16))
    solved[...] = value
    outgoing[0:block] = value.astype(BF16)
    rows = pl.ds((4 + tick) * block, block)
    other_right = given[rows, 0:columns].astype(F32) + given[rows, columns:].astype(F32)
    value = mm(given[4 * block : 5 * block, :], (other_right - other).astype(BF16))
    outgoing[block:] = value.astype(BF16)


def pair_solve(tick, both, right, inverse, given):
    block, columns = right.shape[1:]
    operands = [both, right, inverse, given]
    return pl.pallas_call(
        functools.partial(pair_kernel, tick),
        out_shape=(
            jax.ShapeDtypeStruct((block, columns), F32),
            jax.ShapeDtypeStruct((2 * block, columns), BF16),
        ),
        in_specs=[VMEM] * len(operands),
        out_specs=(VMEM, VMEM),
        compiler_params=params(),
        name="solve",
    )(*operands)


def products(kept, given, own, beside, third, opposite):
    block = third.shape[0]
    near = lax.rem(lax.axis_index("blk"), 2) * (2 * block)

    def part(at):
        return beside[pl.ds(pl.multiple_of(at, block), block), :]

    odd_one, same_one = part(near), part(near + block)
    self_one = own[0:block]
    value = mm(kept[3], self_one)
    value += mm(kept[1], same_one)
    value += mm(kept[2], odd_one)
    value += mm(kept[0], third[...])
    value += mm(kept[4], opposite[...])
    other = mm(given[0:block, :], same_one)
    other += mm(given[block : 2 * block, :], odd_one)
    other += mm(given[2 * block : 3 * block, :], self_one)
    return value, other


def partial_kernel(kept, given, own, beside, third, opposite, sums):
    block = third.shape[0]
    value, other = products(kept, given, own, beside, third, opposite)
    sums[0:block] = value.astype(BF16)
    sums[block:] = other.astype(BF16)


def pack_kernel(kept, handed, given, packed):
    block = packed.shape[1]
    odd = lax.rem(lax.axis_index("blk"), 2)
    for i in range(3):
        packed[i * block : (i + 1) * block, :] = kept[i]
    packed[3 * block : 5 * block, :] = given[0 : 2 * block, :]
    packed[8 * block :, :] = given[3 * block : 4 * block, :]

    @pl.when(odd == 0)
    def _():
        packed[5 * block : 6 * block, :] = kept[3]
        packed[6 * block : 7 * block, :] = handed[2 * block : 3 * block, :]
        packed[7 * block : 8 * block, :] = given[2 * block : 3 * block, :]

    @pl.when(odd == 1)
    def _():
        packed[5 * block : 6 * block, :] = kept[4]
        packed[6 * block : 8 * block, :] = jnp.zeros((2 * block, block), BF16)


def pack(kept, handed, given):
    block = kept.shape[1]
    return pl.pallas_call(
        pack_kernel,
        out_shape=jax.ShapeDtypeStruct((9 * block, block), BF16),
        in_specs=[VMEM] * 3,
        out_specs=VMEM,
        compiler_params=params(),
        name="pack",
    )(kept, handed, given)


def landed_kernel(packed, beside, third, level, sums):
    block = third.shape[0]

    def factor(i):
        return packed[i * block : (i + 1) * block, :]

    odd_one, same_one = beside[0:block], beside[block:]
    first, second = level[0:block], level[block:]
    value = mm(factor(1), same_one)
    value += mm(factor(2), odd_one)
    value += mm(factor(5), first)
    value += mm(factor(6), second)
    value += mm(factor(0), third[...])
    other = mm(factor(3), same_one)
    other += mm(factor(4), odd_one)
    other += mm(factor(7), first)
    other += mm(factor(8), second)
    sums[0:block] = value.astype(BF16)
    sums[block:] = other.astype(BF16)


def landed_sums(packed, beside, third, level):
    return pl.pallas_call(
        landed_kernel,
        out_shape=jax.ShapeDtypeStruct(beside.shape, BF16),
        in_specs=[VMEM] * 4,
        out_specs=VMEM,
        compiler_params=params(),
        name="landed",
    )(packed, beside, third, level)


def last_kernel(ticks, kept, given, own, beside, third, opposite, *refs):
    solved = refs[:ticks]
    exact, sums, outputs, left = refs[ticks:]
    copies = [pltpu.make_async_copy(solved[t], outputs.at[t], left.at[t]) for t in range(ticks)]
    for copy in copies:
        copy.start()
    value, other = products(kept, given, own, beside, third, opposite)
    exact[...] = value
    sums[...] = other.astype(BF16)
    for copy in copies:
        copy.wait()


def partial_sums(operands):
    block, columns = operands[4].shape
    return pl.pallas_call(
        partial_kernel,
        out_shape=jax.ShapeDtypeStruct((2 * block, columns), BF16),
        in_specs=[VMEM] * len(operands),
        out_specs=VMEM,
        compiler_params=params(),
        name="partial",
    )(*operands)


def last_sums(operands, solved):
    block, columns = operands[4].shape
    ticks = len(solved)
    return pl.pallas_call(
        functools.partial(last_kernel, ticks),
        out_shape=(
            jax.ShapeDtypeStruct((block, columns), F32),
            jax.ShapeDtypeStruct((block, columns), BF16),
            jax.ShapeDtypeStruct((ticks, block, columns), F32),
        ),
        in_specs=[VMEM] * (len(operands) + ticks),
        out_specs=(VMEM, VMEM, HBM),
        scratch_shapes=[pltpu.SemaphoreType.DMA((ticks,))],
        compiler_params=params(),
        name="last",
    )(*operands, *solved)


def carry_kernel(exact, both, carry):
    block = exact.shape[0]
    odd = lax.rem(lax.axis_index("blk"), 2)
    theirs = pl.multiple_of((1 - odd) * block, block)
    carry[...] = exact[...] + both[pl.ds(theirs, block), :].astype(F32)


def carry_sum(exact, both):
    return pl.pallas_call(
        carry_kernel,
        out_shape=jax.ShapeDtypeStruct(exact.shape, F32),
        in_specs=[VMEM, VMEM],
        out_specs=VMEM,
        compiler_params=params(),
        name="carry",
    )(exact, both)


def shards(right_side, inverse_diag, factor_blocks, sources, counts, carry_in):
    ticks, block = right_side.shape[0], right_side.shape[1]
    groups, around = lax.axis_size("grp"), lax.axis_size("blk")
    chips = around // 2
    at = lax.axis_index("blk").astype(jnp.int32)
    odd = lax.rem(at, 2)
    chip_pairs = [[2 * c, 2 * c + 1] for c in range(chips)]
    next_pairs = [[2 * c + 1, (2 * c + 2) % around] for c in range(chips)]
    third_pairs = [[2 * c + 1, (2 * c + 4) % around] for c in range(chips)]
    opposite_pairs = [[b, b + chips] for b in range(chips)]

    def paired(value, pairs):
        return lax.all_gather(value, "blk", axis=0, tiled=True, axis_index_groups=pairs)

    def swapped(value, pairs):
        partner = [(a, b) for a, b in pairs] + [(b, a) for a, b in pairs]
        return lax.ppermute(value, "blk", partner)

    solved, own, inverse, right = first_solve(right_side, carry_in, inverse_diag)
    finished = [solved]

    def swapped_pairs(pairs):
        return {a: b for a, b in pairs} | {b: a for a, b in pairs}

    def forward(value, source_of):
        pairs = [
            (g * around + source_of[b], (g + 1) * around + b) for g in range(groups - 1) for b in range(around)
        ]
        return lax.ppermute(value, ("grp", "blk"), pairs)

    level_of = {b: b if b % 2 == 0 else (b + chips) % around for b in range(around)}

    def exchanged(own):
        mine = own[0:block]
        return swapped(mine, third_pairs), swapped(mine, opposite_pairs)

    third, opposite = exchanged(own)
    chip = paired(own, chip_pairs)
    own = jnp.where(odd == 0, chip, jnp.roll(chip, block, 0))
    near = swapped(own, next_pairs)
    held = (own, third, opposite, sources, counts, factor_blocks, inverse, right)
    own, third, opposite, *held = lax.optimization_barrier(held)
    kept, handed = combine(around, *held)
    near, leaving = lax.optimization_barrier((near, handed))
    given = swapped(leaving, chip_pairs)
    beside = jnp.concatenate([near, near], 0)
    sums = partial_sums([kept, given, own, beside, third, opposite])
    sums = lax.ppermute(sums, "grp", [(g, g + 1) for g in range(groups - 1)])
    sums, *held = lax.optimization_barrier((sums, kept, handed, given))
    packed = forward(pack(*held), {b: b for b in range(around)})
    for tick in range(1, ticks):
        solved, own = pair_solve(tick, paired(sums, chip_pairs), right, inverse, given)
        finished.append(solved)
        if tick + 1 < ticks:
            beside = forward(own, swapped_pairs(next_pairs))
            third = forward(own[0:block], swapped_pairs(third_pairs))
            level = forward(own, level_of)
            sums = landed_sums(packed, beside, third, level)
    third, opposite = exchanged(own)
    beside = paired(own, next_pairs)
    exact, crossing, outputs = last_sums([kept, given, own, beside, third, opposite], finished)
    carry = carry_sum(exact, paired(crossing, chip_pairs))
    return (outputs, carry)


def solution(mesh):
    placed = (
        P(None, ("grp", "blk"), None),
        P(("grp", "blk"), None),
        P(("grp", "blk"), None, None, None),
        P(("grp", "blk"), None),
        P(("grp", "blk")),
        P(("grp", "blk"), None),
    )
    return jax.shard_map(
        shards,
        mesh=mesh,
        in_specs=placed,
        out_specs=(P(None, ("grp", "blk"), None), P(("grp", "blk"), None)),
        check_vma=False,
    )
```

```python
import functools

import jax
import jax.numpy as jnp
from jax import lax
from jax.experimental import pallas as pl
from jax.experimental.pallas import tpu as pltpu
from jax.sharding import PartitionSpec as P

F32 = jnp.float32
BF16 = jnp.bfloat16
VMEM = pl.BlockSpec(memory_space=pltpu.VMEM)
SMEM = pl.BlockSpec(memory_space=pltpu.SMEM)
HBM = pl.BlockSpec(memory_space=pltpu.HBM)
LIMIT = 20 * 1024 * 1024


def params():
    return pltpu.CompilerParams(vmem_limit_bytes=LIMIT)


def mm(a, b):
    return jnp.dot(a, b, preferred_element_type=F32)


def combine_kernel(around, count, source_list, blocks, inverse, right, kept, handed, source_here, landing, sums, arrived, small):
    block = inverse.shape[0]
    copy = pltpu.make_async_copy(source_list, source_here, small)
    copy.start()
    own = lax.axis_index("blk")
    sign = 2 * lax.rem(own, 2) - 1

    def copy_of(k):
        return pltpu.make_async_copy(blocks.at[0, k], landing.at[k], arrived.at[k])

    live = count[0]

    def begin(k, carry):
        copy_of(k).start()
        return carry

    lax.fori_loop(0, live, begin, 0)
    sums[...] = jnp.zeros_like(sums)
    handed[4 * block : 5 * block, :] = inverse[...]
    for tick in range(right.shape[0]):
        value = right[tick]
        high = value.astype(BF16)
        rows = pl.ds((5 + tick) * block, block)
        handed[rows, 0 : value.shape[1]] = high
        handed[rows, value.shape[1] :] = (value - high.astype(F32)).astype(BF16)
    copy.wait()

    def add(k, carry):
        copy_of(k).wait()
        offset = lax.rem(source_here[0, k] - own + 3 + around, around) - 3
        turned = offset * sign
        slot = jnp.where(k == 0, 4, jnp.where(turned >= 0, 3 - turned, 8 + turned))
        sums[slot] = sums[slot] + landing[k].astype(F32)
        return carry

    lax.fori_loop(0, live, add, 0)
    for i in range(5):
        kept[i] = sums[i].astype(BF16)
    for i in range(3):
        handed[i * block : (i + 1) * block, :] = sums[5 + i].astype(BF16)
    handed[3 * block : 4 * block, :] = sums[4].astype(BF16)


def in_hbm(value):
    return pltpu.with_memory_space_constraint(value, pltpu.HBM)


def combine(around, sources, counts, factor_blocks, inverse, right):
    slots, block = factor_blocks.shape[1], factor_blocks.shape[2]
    ticks = right.shape[0]
    return pl.pallas_call(
        functools.partial(combine_kernel, around),
        out_shape=(
            jax.ShapeDtypeStruct((5, block, block), BF16),
            jax.ShapeDtypeStruct(((5 + ticks) * block, block), BF16),
        ),
        in_specs=[SMEM, HBM, HBM, VMEM, VMEM],
        out_specs=(VMEM, VMEM),
        scratch_shapes=[
            pltpu.SMEM(sources.shape, jnp.int32),
            pltpu.VMEM((slots, block, block), BF16),
            pltpu.VMEM((8, block, block), F32),
            pltpu.SemaphoreType.DMA((slots,)),
            pltpu.SemaphoreType.DMA,
        ],
        compiler_params=params(),
        cost_estimate=pl.CostEstimate(flops=4_000_000, bytes_accessed=10_000_000, transcendentals=0),
        name="combine",
    )(counts, in_hbm(sources), in_hbm(factor_blocks), inverse, right)


def first_kernel(right, incoming, inverse, solved, outgoing, inverse_here, later_here, right_here, incoming_here, arrived):
    copies = (
        pltpu.make_async_copy(right.at[0], right_here, arrived.at[0]),
        pltpu.make_async_copy(incoming, incoming_here, arrived.at[1]),
        pltpu.make_async_copy(inverse, inverse_here, arrived.at[2]),
        pltpu.make_async_copy(right.at[pl.ds(1, later_here.shape[0])], later_here, arrived.at[3]),
    )
    for copy in copies:
        copy.start()
    for copy in copies[:3]:
        copy.wait()
    value = mm(inverse_here[...], (right_here[...] - incoming_here[...]).astype(BF16))
    solved[...] = value
    outgoing[...] = value.astype(BF16)
    copies[3].wait()


def first_solve(right_side, carry_in, inverse_diag):
    ticks, block, columns = right_side.shape
    return pl.pallas_call(
        first_kernel,
        out_shape=(
            jax.ShapeDtypeStruct((block, columns), F32),
            jax.ShapeDtypeStruct((block, columns), BF16),
            jax.ShapeDtypeStruct((block, block), BF16),
            jax.ShapeDtypeStruct((ticks - 1, block, columns), F32),
        ),
        in_specs=[HBM, HBM, HBM],
        out_specs=(VMEM, VMEM, VMEM, VMEM),
        scratch_shapes=[
            pltpu.VMEM((block, columns), F32),
            pltpu.VMEM((block, columns), F32),
            pltpu.SemaphoreType.DMA((4,)),
        ],
        compiler_params=params(),
        name="first",
    )(in_hbm(right_side), in_hbm(carry_in), in_hbm(inverse_diag))


def pair_kernel(tick, both, right, inverse, given, *refs):
    far = refs[:-2]
    solved, outgoing = refs[-2:]
    block, columns = solved.shape
    odd = lax.rem(lax.axis_index("blk"), 2)
    mine = odd * (2 * block)
    theirs = (1 - odd) * (2 * block)

    def part(at):
        return both[pl.ds(pl.multiple_of(at, block), block), :].astype(F32)

    incoming = part(mine) + part(theirs + block)
    other = part(mine + block) + part(theirs)
    for ref in far:
        incoming += ref[0:block].astype(F32)
        other += ref[block:].astype(F32)
    value = mm(inverse[...], (right[tick - 1] - incoming).astype(BF16))
    solved[...] = value
    outgoing[0:block] = value.astype(BF16)
    rows = pl.ds((4 + tick) * block, block)
    other_right = given[rows, 0:columns].astype(F32) + given[rows, columns:].astype(F32)
    value = mm(given[4 * block : 5 * block, :], (other_right - other).astype(BF16))
    outgoing[block:] = value.astype(BF16)


def pair_solve(tick, both, right, inverse, given, far):
    block, columns = right.shape[1:]
    operands = [both, right, inverse, given] + ([] if far is None else [far])
    return pl.pallas_call(
        functools.partial(pair_kernel, tick),
        out_shape=(
            jax.ShapeDtypeStruct((block, columns), F32),
            jax.ShapeDtypeStruct((2 * block, columns), BF16),
        ),
        in_specs=[VMEM] * len(operands),
        out_specs=(VMEM, VMEM),
        compiler_params=params(),
        name="solve",
    )(*operands)


def products(kept, given, own, beside, third, opposite):
    block = third.shape[0]
    near = lax.rem(lax.axis_index("blk"), 2) * (2 * block)

    def part(at):
        return beside[pl.ds(pl.multiple_of(at, block), block), :]

    odd_one, same_one = part(near), part(near + block)
    self_one = own[0:block]
    value = mm(kept[3], self_one)
    value += mm(kept[1], same_one)
    value += mm(kept[2], odd_one)
    value += mm(kept[0], third[...])
    if opposite is not None:
        value += mm(kept[4], opposite[...])
    other = mm(given[0:block, :], same_one)
    other += mm(given[block : 2 * block, :], odd_one)
    other += mm(given[2 * block : 3 * block, :], self_one)
    return value, other


def partial_kernel(kept, given, own, beside, third, opposite, sums):
    block = third.shape[0]
    value, other = products(kept, given, own, beside, third, opposite)
    sums[0:block] = value.astype(BF16)
    sums[block:] = other.astype(BF16)


def far_kernel(kept, given, own, beside, third, far_sums, sums, leaving):
    block = third.shape[0]
    value, other = products(kept, given, own, beside, third, None)
    sums[0:block] = value.astype(BF16)
    sums[block:] = other.astype(BF16)
    leaving[0:block] = mm(far_sums[0:block, :], own[0:block]).astype(BF16)
    leaving[block:] = mm(far_sums[block:, :], own[block:]).astype(BF16)


def last_kernel(ticks, kept, given, own, beside, third, opposite, *refs):
    solved = refs[:ticks]
    exact, sums, outputs, left = refs[ticks:]
    copies = [pltpu.make_async_copy(solved[t], outputs.at[t], left.at[t]) for t in range(ticks)]
    for copy in copies:
        copy.start()
    value, other = products(kept, given, own, beside, third, opposite)
    exact[...] = value
    sums[...] = other.astype(BF16)
    for copy in copies:
        copy.wait()


def partial_sums(kernel, operands, pairs_out):
    block, columns = operands[4].shape
    return pl.pallas_call(
        kernel,
        out_shape=(jax.ShapeDtypeStruct((2 * block, columns), BF16),) * pairs_out,
        in_specs=[VMEM] * len(operands),
        out_specs=(VMEM,) * pairs_out,
        compiler_params=params(),
        name="partial",
    )(*operands)


def last_sums(operands, solved):
    block, columns = operands[4].shape
    ticks = len(solved)
    return pl.pallas_call(
        functools.partial(last_kernel, ticks),
        out_shape=(
            jax.ShapeDtypeStruct((block, columns), F32),
            jax.ShapeDtypeStruct((block, columns), BF16),
            jax.ShapeDtypeStruct((ticks, block, columns), F32),
        ),
        in_specs=[VMEM] * (len(operands) + ticks),
        out_specs=(VMEM, VMEM, HBM),
        scratch_shapes=[pltpu.SemaphoreType.DMA((ticks,))],
        compiler_params=params(),
        name="last",
    )(*operands, *solved)


def carry_kernel(exact, both, carry):
    block = exact.shape[0]
    odd = lax.rem(lax.axis_index("blk"), 2)
    theirs = pl.multiple_of((1 - odd) * block, block)
    carry[...] = exact[...] + both[pl.ds(theirs, block), :].astype(F32)


def carry_sum(exact, both):
    return pl.pallas_call(
        carry_kernel,
        out_shape=jax.ShapeDtypeStruct(exact.shape, F32),
        in_specs=[VMEM, VMEM],
        out_specs=VMEM,
        compiler_params=params(),
        name="carry",
    )(exact, both)


def shards(right_side, inverse_diag, factor_blocks, sources, counts, carry_in):
    ticks, block = right_side.shape[0], right_side.shape[1]
    groups, around = lax.axis_size("grp"), lax.axis_size("blk")
    chips = around // 2
    at = lax.axis_index("blk").astype(jnp.int32)
    odd = lax.rem(at, 2)
    chip_pairs = [[2 * c, 2 * c + 1] for c in range(chips)]
    next_pairs = [[2 * c + 1, (2 * c + 2) % around] for c in range(chips)]
    third_pairs = [[2 * c + 1, (2 * c + 4) % around] for c in range(chips)]
    opposite_pairs = [[b, b + chips] for b in range(chips)]

    def paired(value, pairs):
        return lax.all_gather(value, "blk", axis=0, tiled=True, axis_index_groups=pairs)

    def swapped(value, pairs):
        partner = [(a, b) for a, b in pairs] + [(b, a) for a, b in pairs]
        return lax.ppermute(value, "blk", partner)

    solved, own, inverse, right = first_solve(right_side, carry_in, inverse_diag)
    finished = [solved]
    far_sums = None
    forward = [(g * around + (b + chips) % around, (g + 1) * around + b) for g in range(groups - 1) for b in range(around)]
    for tick in range(ticks):
        last = tick + 1 == ticks
        near_form = tick == 0 or last
        mine = own[0:block]
        third = swapped(mine, third_pairs)
        opposite = swapped(mine, opposite_pairs) if near_form else None
        if tick == 0:
            chip = paired(own, chip_pairs)
            own = jnp.where(odd == 0, chip, jnp.roll(chip, block, 0))
            held = (own, third, opposite, sources, counts, factor_blocks, inverse, right)
            own, third, opposite, *held = lax.optimization_barrier(held)
            kept, handed = combine(around, *held)
            given = swapped(handed, chip_pairs)
        beside = paired(own, next_pairs)
        operands = [kept, given, own, beside, third]
        if last:
            exact, crossing, outputs = last_sums(operands + [opposite], finished)
            carry = carry_sum(exact, paired(crossing, chip_pairs))
            return (outputs, carry)
        far = None
        if near_form:
            (sums,) = partial_sums(partial_kernel, operands + [opposite], 1)
            own_far, pair_far = lax.optimization_barrier((sums, kept[4], given[3 * block : 4 * block]))[1:]
            far_sums = swapped(jnp.concatenate([own_far, pair_far], 0), opposite_pairs)
        else:
            sums, leaving = partial_sums(far_kernel, operands + [far_sums], 2)
            far = lax.ppermute(leaving, ("grp", "blk"), forward)
        moved = lax.ppermute(sums, "grp", [(g, g + 1) for g in range(groups - 1)])
        both = paired(moved, chip_pairs)
        solved, own = pair_solve(tick + 1, both, right, inverse, given, far)
        finished.append(solved)


def solution(mesh):
    placed = (
        P(None, ("grp", "blk"), None),
        P(("grp", "blk"), None),
        P(("grp", "blk"), None, None, None),
        P(("grp", "blk"), None),
        P(("grp", "blk")),
        P(("grp", "blk"), None),
    )
    return jax.shard_map(
        shards,
        mesh=mesh,
        in_specs=placed,
        out_specs=(P(None, ("grp", "blk"), None), P(("grp", "blk"), None)),
        check_vma=False,
    )
```

```python
import functools

import jax
import jax.numpy as jnp
from jax import lax
from jax.experimental import pallas as pl
from jax.experimental.pallas import tpu as pltpu
from jax.sharding import PartitionSpec as P

F32 = jnp.float32
BF16 = jnp.bfloat16
VMEM = pl.BlockSpec(memory_space=pltpu.VMEM)
SMEM = pl.BlockSpec(memory_space=pltpu.SMEM)
HBM = pl.BlockSpec(memory_space=pltpu.HBM)
LIMIT = 20 * 1024 * 1024


def params():
    return pltpu.CompilerParams(vmem_limit_bytes=LIMIT)


def mm(a, b):
    return jnp.dot(a, b, preferred_element_type=F32)


def combine_kernel(around, count, source_list, blocks, inverse, right, kept, handed, source_here, landing, sums, arrived, small):
    block = inverse.shape[0]
    copy = pltpu.make_async_copy(source_list, source_here, small)
    copy.start()
    own = lax.axis_index("blk")
    sign = 2 * lax.rem(own, 2) - 1

    def copy_of(k):
        return pltpu.make_async_copy(blocks.at[0, k], landing.at[k], arrived.at[k])

    live = count[0]

    def begin(k, carry):
        copy_of(k).start()
        return carry

    lax.fori_loop(0, live, begin, 0)
    sums[...] = jnp.zeros_like(sums)
    handed[4 * block : 5 * block, :] = inverse[...]
    for tick in range(right.shape[0]):
        value = right[tick]
        high = value.astype(BF16)
        rows = pl.ds((5 + tick) * block, block)
        handed[rows, 0 : value.shape[1]] = high
        handed[rows, value.shape[1] :] = (value - high.astype(F32)).astype(BF16)
    copy.wait()

    def add(k, carry):
        copy_of(k).wait()
        offset = lax.rem(source_here[0, k] - own + 3 + around, around) - 3
        turned = offset * sign
        slot = jnp.where(k == 0, 4, jnp.where(turned >= 0, 3 - turned, 8 + turned))
        sums[slot] = sums[slot] + landing[k].astype(F32)
        return carry

    lax.fori_loop(0, live, add, 0)
    for i in range(5):
        kept[i] = sums[i].astype(BF16)
    for i in range(3):
        handed[i * block : (i + 1) * block, :] = sums[5 + i].astype(BF16)
    handed[3 * block : 4 * block, :] = sums[4].astype(BF16)


def in_hbm(value):
    return pltpu.with_memory_space_constraint(value, pltpu.HBM)


def combine(around, sources, counts, factor_blocks, inverse, right):
    slots, block = factor_blocks.shape[1], factor_blocks.shape[2]
    ticks = right.shape[0]
    return pl.pallas_call(
        functools.partial(combine_kernel, around),
        out_shape=(
            jax.ShapeDtypeStruct((5, block, block), BF16),
            jax.ShapeDtypeStruct(((5 + ticks) * block, block), BF16),
        ),
        in_specs=[SMEM, HBM, HBM, VMEM, VMEM],
        out_specs=(VMEM, VMEM),
        scratch_shapes=[
            pltpu.SMEM(sources.shape, jnp.int32),
            pltpu.VMEM((slots, block, block), BF16),
            pltpu.VMEM((8, block, block), F32),
            pltpu.SemaphoreType.DMA((slots,)),
            pltpu.SemaphoreType.DMA,
        ],
        compiler_params=params(),
        cost_estimate=pl.CostEstimate(flops=4_000_000, bytes_accessed=10_000_000, transcendentals=0),
        name="combine",
    )(counts, in_hbm(sources), in_hbm(factor_blocks), inverse, right)


def first_kernel(right, incoming, inverse, solved, outgoing, inverse_here, later_here, right_here, incoming_here, arrived):
    copies = (
        pltpu.make_async_copy(right.at[0], right_here, arrived.at[0]),
        pltpu.make_async_copy(incoming, incoming_here, arrived.at[1]),
        pltpu.make_async_copy(inverse, inverse_here, arrived.at[2]),
        pltpu.make_async_copy(right.at[pl.ds(1, later_here.shape[0])], later_here, arrived.at[3]),
    )
    for copy in copies:
        copy.start()
    for copy in copies[:3]:
        copy.wait()
    value = mm(inverse_here[...], (right_here[...] - incoming_here[...]).astype(BF16))
    solved[...] = value
    outgoing[...] = value.astype(BF16)
    copies[3].wait()


def first_solve(right_side, carry_in, inverse_diag):
    ticks, block, columns = right_side.shape
    return pl.pallas_call(
        first_kernel,
        out_shape=(
            jax.ShapeDtypeStruct((block, columns), F32),
            jax.ShapeDtypeStruct((block, columns), BF16),
            jax.ShapeDtypeStruct((block, block), BF16),
            jax.ShapeDtypeStruct((ticks - 1, block, columns), F32),
        ),
        in_specs=[HBM, HBM, HBM],
        out_specs=(VMEM, VMEM, VMEM, VMEM),
        scratch_shapes=[
            pltpu.VMEM((block, columns), F32),
            pltpu.VMEM((block, columns), F32),
            pltpu.SemaphoreType.DMA((4,)),
        ],
        compiler_params=params(),
        name="first",
    )(in_hbm(right_side), in_hbm(carry_in), in_hbm(inverse_diag))


def pair_kernel(tick, both, right, inverse, given, solved, outgoing):
    block, columns = solved.shape
    odd = lax.rem(lax.axis_index("blk"), 2)
    rows = both.shape[0] // 2
    mine = odd * rows
    theirs = (1 - odd) * rows

    def part(at):
        return both[pl.ds(pl.multiple_of(at, block), block), :].astype(F32)

    incoming = part(mine) + part(theirs + block)
    other = part(mine + block) + part(theirs)
    for i in range(2 * block, rows, 2 * block):
        incoming += part(mine + i) + part(theirs + i + block)
        other += part(mine + i + block) + part(theirs + i)
    value = mm(inverse[...], (right[tick - 1] - incoming).astype(BF16))
    solved[...] = value
    outgoing[0:block] = value.astype(BF16)
    rows = pl.ds((4 + tick) * block, block)
    other_right = given[rows, 0:columns].astype(F32) + given[rows, columns:].astype(F32)
    value = mm(given[4 * block : 5 * block, :], (other_right - other).astype(BF16))
    outgoing[block:] = value.astype(BF16)


def pair_solve(tick, both, right, inverse, given):
    block, columns = right.shape[1:]
    operands = [both, right, inverse, given]
    return pl.pallas_call(
        functools.partial(pair_kernel, tick),
        out_shape=(
            jax.ShapeDtypeStruct((block, columns), F32),
            jax.ShapeDtypeStruct((2 * block, columns), BF16),
        ),
        in_specs=[VMEM] * len(operands),
        out_specs=(VMEM, VMEM),
        compiler_params=params(),
        name="solve",
    )(*operands)


def products(kept, given, own, beside, third, opposite):
    block = third.shape[0]
    near = lax.rem(lax.axis_index("blk"), 2) * (2 * block)

    def part(at):
        return beside[pl.ds(pl.multiple_of(at, block), block), :]

    odd_one, same_one = part(near), part(near + block)
    self_one = own[0:block]
    value = mm(kept[3], self_one)
    value += mm(kept[1], same_one)
    value += mm(kept[2], odd_one)
    value += mm(kept[0], third[...])
    if opposite is not None:
        value += mm(kept[4], opposite[0:block])
    other = mm(given[0:block, :], same_one)
    other += mm(given[block : 2 * block, :], odd_one)
    other += mm(given[2 * block : 3 * block, :], self_one)
    if opposite is not None:
        other += mm(given[3 * block : 4 * block, :], opposite[block:])
    return value, other


def partial_kernel(kept, given, own, beside, third, opposite, sums):
    block = third.shape[0]
    value, other = products(kept, given, own, beside, third, opposite)
    sums[0:block] = value.astype(BF16)
    sums[block:] = other.astype(BF16)


def far_kernel(kept, given, own, beside, third, far_sums, sums, leaving):
    block = third.shape[0]
    value, other = products(kept, given, own, beside, third, None)
    sums[0:block] = value.astype(BF16)
    sums[block:] = other.astype(BF16)
    leaving[0:block] = mm(far_sums[0:block, :], own[0:block]).astype(BF16)
    leaving[block:] = mm(far_sums[block:, :], own[block:]).astype(BF16)


def last_kernel(ticks, kept, given, own, beside, third, opposite, *refs):
    solved = refs[:ticks]
    exact, sums, outputs, left = refs[ticks:]
    copies = [pltpu.make_async_copy(solved[t], outputs.at[t], left.at[t]) for t in range(ticks)]
    for copy in copies:
        copy.start()
    value, other = products(kept, given, own, beside, third, opposite)
    exact[...] = value
    sums[...] = other.astype(BF16)
    for copy in copies:
        copy.wait()


def partial_sums(kernel, operands, pairs_out):
    block, columns = operands[4].shape
    return pl.pallas_call(
        kernel,
        out_shape=(jax.ShapeDtypeStruct((2 * block, columns), BF16),) * pairs_out,
        in_specs=[VMEM] * len(operands),
        out_specs=(VMEM,) * pairs_out,
        compiler_params=params(),
        name="partial",
    )(*operands)


def last_sums(operands, solved):
    block, columns = operands[4].shape
    ticks = len(solved)
    return pl.pallas_call(
        functools.partial(last_kernel, ticks),
        out_shape=(
            jax.ShapeDtypeStruct((block, columns), F32),
            jax.ShapeDtypeStruct((block, columns), BF16),
            jax.ShapeDtypeStruct((ticks, block, columns), F32),
        ),
        in_specs=[VMEM] * (len(operands) + ticks),
        out_specs=(VMEM, VMEM, HBM),
        scratch_shapes=[pltpu.SemaphoreType.DMA((ticks,))],
        compiler_params=params(),
        name="last",
    )(*operands, *solved)


def carry_kernel(exact, both, carry):
    block = exact.shape[0]
    odd = lax.rem(lax.axis_index("blk"), 2)
    theirs = pl.multiple_of((1 - odd) * block, block)
    carry[...] = exact[...] + both[pl.ds(theirs, block), :].astype(F32)


def carry_sum(exact, both):
    return pl.pallas_call(
        carry_kernel,
        out_shape=jax.ShapeDtypeStruct(exact.shape, F32),
        in_specs=[VMEM, VMEM],
        out_specs=VMEM,
        compiler_params=params(),
        name="carry",
    )(exact, both)


def shards(right_side, inverse_diag, factor_blocks, sources, counts, carry_in):
    ticks, block = right_side.shape[0], right_side.shape[1]
    groups, around = lax.axis_size("grp"), lax.axis_size("blk")
    chips = around // 2
    at = lax.axis_index("blk").astype(jnp.int32)
    odd = lax.rem(at, 2)
    chip_pairs = [[2 * c, 2 * c + 1] for c in range(chips)]
    next_pairs = [[2 * c + 1, (2 * c + 2) % around] for c in range(chips)]
    third_pairs = [[2 * c + 1, (2 * c + 4) % around] for c in range(chips)]
    opposite_pairs = [[b, b + chips] for b in range(chips)]

    def paired(value, pairs):
        return lax.all_gather(value, "blk", axis=0, tiled=True, axis_index_groups=pairs)

    def swapped(value, pairs):
        partner = [(a, b) for a, b in pairs] + [(b, a) for a, b in pairs]
        return lax.ppermute(value, "blk", partner)

    solved, own, inverse, right = first_solve(right_side, carry_in, inverse_diag)
    finished = [solved]
    far_sums = None
    seconds = range(1, around, 2)
    opposite_of = [(b, (b + chips) % around) for b in seconds]
    forward = [(g * around + a, (g + 1) * around + b) for g in range(groups - 1) for a, b in opposite_of]
    for tick in range(ticks):
        last = tick + 1 == ticks
        near_form = tick == 0 or last
        third = swapped(own[0:block], third_pairs)
        if tick == 0:
            chip = paired(own, chip_pairs)
            own = jnp.where(odd == 0, chip, jnp.roll(chip, block, 0))
            held = lax.optimization_barrier((own, sources, counts, factor_blocks, inverse, right))[1:]
            kept, handed = combine(around, *held)
            given = swapped(handed, chip_pairs)
        opposite = lax.ppermute(own, "blk", opposite_of) if near_form else None
        beside = paired(own, next_pairs)
        operands = [kept, given, own, beside, third]
        if last:
            exact, crossing, outputs = last_sums(operands + [opposite], finished)
            carry = carry_sum(exact, paired(crossing, chip_pairs))
            return (outputs, carry)
        if near_form:
            (sums,) = partial_sums(partial_kernel, operands + [opposite], 1)
            own_far, pair_far = lax.optimization_barrier((sums, kept[4], given[3 * block : 4 * block]))[1:]
            far_sums = lax.ppermute(jnp.concatenate([own_far, pair_far], 0), "blk", opposite_of)
        else:
            sums, leaving = partial_sums(far_kernel, operands + [far_sums], 2)
            far = lax.ppermute(leaving, ("grp", "blk"), forward)
        sums = lax.ppermute(sums, "grp", [(g, g + 1) for g in range(groups - 1)])
        if not near_form:
            sums = jnp.concatenate([sums, far], 0)
        solved, own = pair_solve(tick + 1, paired(sums, chip_pairs), right, inverse, given)
        finished.append(solved)


def solution(mesh):
    placed = (
        P(None, ("grp", "blk"), None),
        P(("grp", "blk"), None),
        P(("grp", "blk"), None, None, None),
        P(("grp", "blk"), None),
        P(("grp", "blk")),
        P(("grp", "blk"), None),
    )
    return jax.shard_map(
        shards,
        mesh=mesh,
        in_specs=placed,
        out_specs=(P(None, ("grp", "blk"), None), P(("grp", "blk"), None)),
        check_vma=False,
    )
```

```python
import functools

import jax
import jax.numpy as jnp
from jax import lax
from jax.experimental import pallas as pl
from jax.experimental.pallas import tpu as pltpu
from jax.sharding import PartitionSpec as P

F32 = jnp.float32
BF16 = jnp.bfloat16
VMEM = pl.BlockSpec(memory_space=pltpu.VMEM)
SMEM = pl.BlockSpec(memory_space=pltpu.SMEM)
HBM = pl.BlockSpec(memory_space=pltpu.HBM)
LIMIT = 20 * 1024 * 1024


def params():
    return pltpu.CompilerParams(vmem_limit_bytes=LIMIT)


def mm(a, b):
    return jnp.dot(a, b, preferred_element_type=F32)


def combine_kernel(around, count, source_list, blocks, inverse, right, kept, handed, source_here, landing, sums, arrived, small):
    block = inverse.shape[0]
    copy = pltpu.make_async_copy(source_list, source_here, small)
    copy.start()
    own = lax.axis_index("blk")
    sign = 2 * lax.rem(own, 2) - 1

    def copy_of(k):
        return pltpu.make_async_copy(blocks.at[0, k], landing.at[k], arrived.at[k])

    live = count[0]

    def begin(k, carry):
        copy_of(k).start()
        return carry

    lax.fori_loop(0, live, begin, 0)
    sums[...] = jnp.zeros_like(sums)
    handed[4 * block : 5 * block, :] = inverse[...]
    for tick in range(right.shape[0]):
        value = right[tick]
        high = value.astype(BF16)
        rows = pl.ds((5 + tick) * block, block)
        handed[rows, 0 : value.shape[1]] = high
        handed[rows, value.shape[1] :] = (value - high.astype(F32)).astype(BF16)
    copy.wait()

    def add(k, carry):
        copy_of(k).wait()
        offset = lax.rem(source_here[0, k] - own + 3 + around, around) - 3
        turned = offset * sign
        slot = jnp.where(k == 0, 4, jnp.where(turned >= 0, 3 - turned, 8 + turned))
        sums[slot] = sums[slot] + landing[k].astype(F32)
        return carry

    lax.fori_loop(0, live, add, 0)
    for i in range(5):
        kept[i] = sums[i].astype(BF16)
    for i in range(3):
        handed[i * block : (i + 1) * block, :] = sums[5 + i].astype(BF16)
    handed[3 * block : 4 * block, :] = sums[4].astype(BF16)


def in_hbm(value):
    return pltpu.with_memory_space_constraint(value, pltpu.HBM)


def combine(around, sources, counts, factor_blocks, inverse, right):
    slots, block = factor_blocks.shape[1], factor_blocks.shape[2]
    ticks = right.shape[0]
    return pl.pallas_call(
        functools.partial(combine_kernel, around),
        out_shape=(
            jax.ShapeDtypeStruct((5, block, block), BF16),
            jax.ShapeDtypeStruct(((5 + ticks) * block, block), BF16),
        ),
        in_specs=[SMEM, HBM, HBM, VMEM, VMEM],
        out_specs=(VMEM, VMEM),
        scratch_shapes=[
            pltpu.SMEM(sources.shape, jnp.int32),
            pltpu.VMEM((slots, block, block), BF16),
            pltpu.VMEM((8, block, block), F32),
            pltpu.SemaphoreType.DMA((slots,)),
            pltpu.SemaphoreType.DMA,
        ],
        compiler_params=params(),
        cost_estimate=pl.CostEstimate(flops=4_000_000, bytes_accessed=10_000_000, transcendentals=0),
        name="combine",
    )(counts, in_hbm(sources), in_hbm(factor_blocks), inverse, right)


def first_kernel(right, incoming, inverse, solved, outgoing, inverse_here, later_here, right_here, incoming_here, arrived):
    copies = (
        pltpu.make_async_copy(right.at[0], right_here, arrived.at[0]),
        pltpu.make_async_copy(incoming, incoming_here, arrived.at[1]),
        pltpu.make_async_copy(inverse, inverse_here, arrived.at[2]),
        pltpu.make_async_copy(right.at[pl.ds(1, later_here.shape[0])], later_here, arrived.at[3]),
    )
    for copy in copies:
        copy.start()
    for copy in copies[:3]:
        copy.wait()
    value = mm(inverse_here[...], (right_here[...] - incoming_here[...]).astype(BF16))
    solved[...] = value
    outgoing[...] = value.astype(BF16)
    copies[3].wait()


def first_solve(right_side, carry_in, inverse_diag):
    ticks, block, columns = right_side.shape
    return pl.pallas_call(
        first_kernel,
        out_shape=(
            jax.ShapeDtypeStruct((block, columns), F32),
            jax.ShapeDtypeStruct((block, columns), BF16),
            jax.ShapeDtypeStruct((block, block), BF16),
            jax.ShapeDtypeStruct((ticks - 1, block, columns), F32),
        ),
        in_specs=[HBM, HBM, HBM],
        out_specs=(VMEM, VMEM, VMEM, VMEM),
        scratch_shapes=[
            pltpu.VMEM((block, columns), F32),
            pltpu.VMEM((block, columns), F32),
            pltpu.SemaphoreType.DMA((4,)),
        ],
        compiler_params=params(),
        name="first",
    )(in_hbm(right_side), in_hbm(carry_in), in_hbm(inverse_diag))


def pair_kernel(tick, both, right, inverse, given, *refs):
    far = refs[:-3]
    solved, outgoing, alone = refs[-3:]
    block, columns = solved.shape
    odd = lax.rem(lax.axis_index("blk"), 2)
    mine = odd * (2 * block)
    theirs = (1 - odd) * (2 * block)

    def part(at):
        return both[pl.ds(pl.multiple_of(at, block), block), :].astype(F32)

    incoming = part(mine) + part(theirs + block)
    other = part(mine + block) + part(theirs)
    for ref in far:
        incoming += ref[0:block].astype(F32)
        other += ref[block:].astype(F32)
    value = mm(inverse[...], (right[tick - 1] - incoming).astype(BF16))
    solved[...] = value
    outgoing[0:block] = value.astype(BF16)
    alone[...] = value.astype(BF16)
    rows = pl.ds((4 + tick) * block, block)
    other_right = given[rows, 0:columns].astype(F32) + given[rows, columns:].astype(F32)
    value = mm(given[4 * block : 5 * block, :], (other_right - other).astype(BF16))
    outgoing[block:] = value.astype(BF16)


def pair_solve(tick, both, right, inverse, given, far):
    block, columns = right.shape[1:]
    operands = [both, right, inverse, given] + ([] if far is None else [far])
    return pl.pallas_call(
        functools.partial(pair_kernel, tick),
        out_shape=(
            jax.ShapeDtypeStruct((block, columns), F32),
            jax.ShapeDtypeStruct((2 * block, columns), BF16),
            jax.ShapeDtypeStruct((block, columns), BF16),
        ),
        in_specs=[VMEM] * len(operands),
        out_specs=(VMEM, VMEM, VMEM),
        compiler_params=params(),
        name="solve",
    )(*operands)


def products(kept, given, own, beside, third, opposite):
    block = third.shape[0]
    near = lax.rem(lax.axis_index("blk"), 2) * (2 * block)

    def part(at):
        return beside[pl.ds(pl.multiple_of(at, block), block), :]

    odd_one, same_one = part(near), part(near + block)
    self_one = own[0:block]
    value = mm(kept[3], self_one)
    value += mm(kept[1], same_one)
    value += mm(kept[2], odd_one)
    value += mm(kept[0], third[...])
    if opposite is not None:
        value += mm(kept[4], opposite[0:block])
    other = mm(given[0:block, :], same_one)
    other += mm(given[block : 2 * block, :], odd_one)
    other += mm(given[2 * block : 3 * block, :], self_one)
    if opposite is not None:
        other += mm(given[3 * block : 4 * block, :], opposite[block:])
    return value, other


def partial_kernel(kept, given, own, beside, third, opposite, sums):
    block = third.shape[0]
    value, other = products(kept, given, own, beside, third, opposite)
    sums[0:block] = value.astype(BF16)
    sums[block:] = other.astype(BF16)


def far_kernel(kept, given, own, beside, third, far_sums, sums, leaving):
    block = third.shape[0]
    value, other = products(kept, given, own, beside, third, None)
    sums[0:block] = value.astype(BF16)
    sums[block:] = other.astype(BF16)
    leaving[0:block] = mm(far_sums[0:block, :], own[0:block]).astype(BF16)
    leaving[block:] = mm(far_sums[block:, :], own[block:]).astype(BF16)


def last_kernel(ticks, kept, given, own, beside, third, opposite, *refs):
    solved = refs[:ticks]
    exact, sums, outputs, left = refs[ticks:]
    copies = [pltpu.make_async_copy(solved[t], outputs.at[t], left.at[t]) for t in range(ticks)]
    for copy in copies:
        copy.start()
    value, other = products(kept, given, own, beside, third, opposite)
    exact[...] = value
    sums[...] = other.astype(BF16)
    for copy in copies:
        copy.wait()


def partial_sums(kernel, operands, pairs_out):
    block, columns = operands[4].shape
    return pl.pallas_call(
        kernel,
        out_shape=(jax.ShapeDtypeStruct((2 * block, columns), BF16),) * pairs_out,
        in_specs=[VMEM] * len(operands),
        out_specs=(VMEM,) * pairs_out,
        compiler_params=params(),
        name="partial",
    )(*operands)


def last_sums(operands, solved):
    block, columns = operands[4].shape
    ticks = len(solved)
    return pl.pallas_call(
        functools.partial(last_kernel, ticks),
        out_shape=(
            jax.ShapeDtypeStruct((block, columns), F32),
            jax.ShapeDtypeStruct((block, columns), BF16),
            jax.ShapeDtypeStruct((ticks, block, columns), F32),
        ),
        in_specs=[VMEM] * (len(operands) + ticks),
        out_specs=(VMEM, VMEM, HBM),
        scratch_shapes=[pltpu.SemaphoreType.DMA((ticks,))],
        compiler_params=params(),
        name="last",
    )(*operands, *solved)


def carry_kernel(exact, both, carry):
    block = exact.shape[0]
    odd = lax.rem(lax.axis_index("blk"), 2)
    theirs = pl.multiple_of((1 - odd) * block, block)
    carry[...] = exact[...] + both[pl.ds(theirs, block), :].astype(F32)


def carry_sum(exact, both):
    return pl.pallas_call(
        carry_kernel,
        out_shape=jax.ShapeDtypeStruct(exact.shape, F32),
        in_specs=[VMEM, VMEM],
        out_specs=VMEM,
        compiler_params=params(),
        name="carry",
    )(exact, both)


def shards(right_side, inverse_diag, factor_blocks, sources, counts, carry_in):
    ticks, block = right_side.shape[0], right_side.shape[1]
    groups, around = lax.axis_size("grp"), lax.axis_size("blk")
    chips = around // 2
    at = lax.axis_index("blk").astype(jnp.int32)
    odd = lax.rem(at, 2)
    chip_pairs = [[2 * c, 2 * c + 1] for c in range(chips)]
    next_pairs = [[2 * c + 1, (2 * c + 2) % around] for c in range(chips)]
    third_pairs = [[2 * c + 1, (2 * c + 4) % around] for c in range(chips)]
    opposite_pairs = [[b, b + chips] for b in range(chips)]

    def paired(value, pairs):
        return lax.all_gather(value, "blk", axis=0, tiled=True, axis_index_groups=pairs)

    def swapped(value, pairs):
        partner = [(a, b) for a, b in pairs] + [(b, a) for a, b in pairs]
        return lax.ppermute(value, "blk", partner)

    solved, own, inverse, right = first_solve(right_side, carry_in, inverse_diag)
    finished = [solved]
    far_sums = None
    seconds = [(b, (b + chips) % around) for b in range(1, around, 2)]
    forward = [(g * around + (b + chips) % around, (g + 1) * around + b) for g in range(groups - 1) for b in range(around)]
    mine = own
    for tick in range(ticks):
        last = tick + 1 == ticks
        near_form = tick == 0 or last
        third = swapped(own if last else mine, third_pairs)[0:block]
        if tick == 0:
            chip = paired(mine, chip_pairs)
            own = jnp.where(odd == 0, chip, jnp.roll(chip, block, 0))
            held = lax.optimization_barrier((own, sources, counts, factor_blocks, inverse, right))[1:]
            kept, handed = combine(around, *held)
            given = swapped(handed, chip_pairs)
        opposite = None
        if near_form:
            turned = jnp.where(odd == 1, own, jnp.zeros_like(own)) if tick == 0 else own
            opposite = lax.ppermute(turned, "blk", seconds)
        beside = paired(own, next_pairs)
        operands = [kept, given, own, beside, third]
        if last:
            exact, crossing, outputs = last_sums(operands + [opposite], finished)
            carry = carry_sum(exact, paired(crossing, chip_pairs))
            return (outputs, carry)
        far = None
        if near_form:
            (sums,) = partial_sums(partial_kernel, operands + [opposite], 1)
            own_far, pair_far = lax.optimization_barrier((sums, kept[4], given[3 * block : 4 * block]))[1:]
            far_sums = swapped(jnp.concatenate([own_far, pair_far], 0), opposite_pairs)
        else:
            sums, leaving = partial_sums(far_kernel, operands + [far_sums], 2)
            far = lax.ppermute(leaving, ("grp", "blk"), forward)
        moved = lax.ppermute(sums, "grp", [(g, g + 1) for g in range(groups - 1)])
        both = paired(moved, chip_pairs)
        solved, own, mine = pair_solve(tick + 1, both, right, inverse, given, far)
        finished.append(solved)


def solution(mesh):
    placed = (
        P(None, ("grp", "blk"), None),
        P(("grp", "blk"), None),
        P(("grp", "blk"), None, None, None),
        P(("grp", "blk"), None),
        P(("grp", "blk")),
        P(("grp", "blk"), None),
    )
    return jax.shard_map(
        shards,
        mesh=mesh,
        in_specs=placed,
        out_specs=(P(None, ("grp", "blk"), None), P(("grp", "blk"), None)),
        check_vma=False,
    )
```

```python
import functools

import jax
import jax.numpy as jnp
from jax import lax
from jax.experimental import pallas as pl
from jax.experimental.pallas import tpu as pltpu
from jax.sharding import PartitionSpec as P

F32 = jnp.float32
BF16 = jnp.bfloat16
VMEM = pl.BlockSpec(memory_space=pltpu.VMEM)
SMEM = pl.BlockSpec(memory_space=pltpu.SMEM)
HBM = pl.BlockSpec(memory_space=pltpu.HBM)
LIMIT = 20 * 1024 * 1024


def params():
    return pltpu.CompilerParams(vmem_limit_bytes=LIMIT)


def mm(a, b):
    return jnp.dot(a, b, preferred_element_type=F32)


def combine_kernel(around, count, source_list, blocks, inverse, right, kept, handed, source_here, landing, sums, arrived, small):
    block = inverse.shape[0]
    copy = pltpu.make_async_copy(source_list, source_here, small)
    copy.start()
    own = lax.axis_index("blk")
    sign = 2 * lax.rem(own, 2) - 1

    def copy_of(k):
        return pltpu.make_async_copy(blocks.at[0, k], landing.at[k], arrived.at[k])

    live = count[0]

    def begin(k, carry):
        copy_of(k).start()
        return carry

    lax.fori_loop(0, live, begin, 0)
    sums[...] = jnp.zeros_like(sums)
    handed[4 * block : 5 * block, :] = inverse[...]
    for tick in range(right.shape[0]):
        value = right[tick]
        high = value.astype(BF16)
        rows = pl.ds((5 + tick) * block, block)
        handed[rows, 0 : value.shape[1]] = high
        handed[rows, value.shape[1] :] = (value - high.astype(F32)).astype(BF16)
    copy.wait()

    def add(k, carry):
        copy_of(k).wait()
        offset = lax.rem(source_here[0, k] - own + 3 + around, around) - 3
        turned = offset * sign
        slot = jnp.where(k == 0, 4, jnp.where(turned >= 0, 3 - turned, 8 + turned))
        sums[slot] = sums[slot] + landing[k].astype(F32)
        return carry

    lax.fori_loop(0, live, add, 0)
    for i in range(5):
        kept[i] = sums[i].astype(BF16)
    for i in range(3):
        handed[i * block : (i + 1) * block, :] = sums[5 + i].astype(BF16)
    handed[3 * block : 4 * block, :] = sums[4].astype(BF16)


def in_hbm(value):
    return pltpu.with_memory_space_constraint(value, pltpu.HBM)


def combine(around, sources, counts, factor_blocks, inverse, right):
    slots, block = factor_blocks.shape[1], factor_blocks.shape[2]
    ticks = right.shape[0]
    return pl.pallas_call(
        functools.partial(combine_kernel, around),
        out_shape=(
            jax.ShapeDtypeStruct((5, block, block), BF16),
            jax.ShapeDtypeStruct(((5 + ticks) * block, block), BF16),
        ),
        in_specs=[SMEM, HBM, HBM, VMEM, VMEM],
        out_specs=(VMEM, VMEM),
        scratch_shapes=[
            pltpu.SMEM(sources.shape, jnp.int32),
            pltpu.VMEM((slots, block, block), BF16),
            pltpu.VMEM((8, block, block), F32),
            pltpu.SemaphoreType.DMA((slots,)),
            pltpu.SemaphoreType.DMA,
        ],
        compiler_params=params(),
        cost_estimate=pl.CostEstimate(flops=4_000_000, bytes_accessed=10_000_000, transcendentals=0),
        name="combine",
    )(counts, in_hbm(sources), in_hbm(factor_blocks), inverse, right)


def first_kernel(right, incoming, inverse, solved, outgoing, inverse_here, later_here, right_here, incoming_here, arrived):
    copies = (
        pltpu.make_async_copy(right.at[0], right_here, arrived.at[0]),
        pltpu.make_async_copy(incoming, incoming_here, arrived.at[1]),
        pltpu.make_async_copy(inverse, inverse_here, arrived.at[2]),
        pltpu.make_async_copy(right.at[pl.ds(1, later_here.shape[0])], later_here, arrived.at[3]),
    )
    for copy in copies:
        copy.start()
    for copy in copies[:3]:
        copy.wait()
    value = mm(inverse_here[...], (right_here[...] - incoming_here[...]).astype(BF16))
    solved[...] = value
    outgoing[...] = value.astype(BF16)
    copies[3].wait()


def first_solve(right_side, carry_in, inverse_diag):
    ticks, block, columns = right_side.shape
    return pl.pallas_call(
        first_kernel,
        out_shape=(
            jax.ShapeDtypeStruct((block, columns), F32),
            jax.ShapeDtypeStruct((block, columns), BF16),
            jax.ShapeDtypeStruct((block, block), BF16),
            jax.ShapeDtypeStruct((ticks - 1, block, columns), F32),
        ),
        in_specs=[HBM, HBM, HBM],
        out_specs=(VMEM, VMEM, VMEM, VMEM),
        scratch_shapes=[
            pltpu.VMEM((block, columns), F32),
            pltpu.VMEM((block, columns), F32),
            pltpu.SemaphoreType.DMA((4,)),
        ],
        compiler_params=params(),
        name="first",
    )(in_hbm(right_side), in_hbm(carry_in), in_hbm(inverse_diag))


def pair_kernel(tick, both, right, inverse, given, solved, outgoing):
    block, columns = solved.shape
    odd = lax.rem(lax.axis_index("blk"), 2)
    mine = odd * (2 * block)
    theirs = (1 - odd) * (2 * block)

    def part(at):
        return both[pl.ds(pl.multiple_of(at, block), block), :].astype(F32)

    incoming = part(mine) + part(theirs + block)
    other = part(mine + block) + part(theirs)
    value = mm(inverse[...], (right[tick - 1] - incoming).astype(BF16))
    solved[...] = value
    outgoing[0:block] = value.astype(BF16)
    rows = pl.ds((4 + tick) * block, block)
    other_right = given[rows, 0:columns].astype(F32) + given[rows, columns:].astype(F32)
    value = mm(given[4 * block : 5 * block, :], (other_right - other).astype(BF16))
    outgoing[block:] = value.astype(BF16)


def pair_solve(tick, both, right, inverse, given):
    block, columns = right.shape[1:]
    operands = [both, right, inverse, given]
    return pl.pallas_call(
        functools.partial(pair_kernel, tick),
        out_shape=(
            jax.ShapeDtypeStruct((block, columns), F32),
            jax.ShapeDtypeStruct((2 * block, columns), BF16),
        ),
        in_specs=[VMEM] * len(operands),
        out_specs=(VMEM, VMEM),
        compiler_params=params(),
        name="solve",
    )(*operands)


def products(kept, given, own, beside, third, opposite):
    block = third.shape[0]
    near = lax.rem(lax.axis_index("blk"), 2) * (2 * block)

    def part(at):
        return beside[pl.ds(pl.multiple_of(at, block), block), :]

    odd_one, same_one = part(near), part(near + block)
    self_one = own[0:block]
    value = mm(kept[3], self_one)
    value += mm(kept[1], same_one)
    value += mm(kept[2], odd_one)
    value += mm(kept[0], third[...])
    value += mm(kept[4], opposite[0:block])
    other = mm(given[0:block, :], same_one)
    other += mm(given[block : 2 * block, :], odd_one)
    other += mm(given[2 * block : 3 * block, :], self_one)
    other += mm(given[3 * block : 4 * block, :], opposite[block:])
    return value, other


def partial_kernel(kept, given, own, beside, third, opposite, sums):
    block = third.shape[0]
    value, other = products(kept, given, own, beside, third, opposite)
    sums[0:block] = value.astype(BF16)
    sums[block:] = other.astype(BF16)


def last_kernel(ticks, kept, given, own, beside, third, opposite, *refs):
    solved = refs[:ticks]
    exact, sums, outputs, left = refs[ticks:]
    copies = [pltpu.make_async_copy(solved[t], outputs.at[t], left.at[t]) for t in range(ticks)]
    for copy in copies:
        copy.start()
    value, other = products(kept, given, own, beside, third, opposite)
    exact[...] = value
    sums[...] = other.astype(BF16)
    for copy in copies:
        copy.wait()


def partial_sums(operands):
    block, columns = operands[4].shape
    return pl.pallas_call(
        partial_kernel,
        out_shape=jax.ShapeDtypeStruct((2 * block, columns), BF16),
        in_specs=[VMEM] * len(operands),
        out_specs=VMEM,
        compiler_params=params(),
        name="partial",
    )(*operands)


def last_sums(operands, solved):
    block, columns = operands[4].shape
    ticks = len(solved)
    return pl.pallas_call(
        functools.partial(last_kernel, ticks),
        out_shape=(
            jax.ShapeDtypeStruct((block, columns), F32),
            jax.ShapeDtypeStruct((block, columns), BF16),
            jax.ShapeDtypeStruct((ticks, block, columns), F32),
        ),
        in_specs=[VMEM] * (len(operands) + ticks),
        out_specs=(VMEM, VMEM, HBM),
        scratch_shapes=[pltpu.SemaphoreType.DMA((ticks,))],
        compiler_params=params(),
        name="last",
    )(*operands, *solved)


def carry_kernel(exact, both, carry):
    block = exact.shape[0]
    odd = lax.rem(lax.axis_index("blk"), 2)
    theirs = pl.multiple_of((1 - odd) * block, block)
    carry[...] = exact[...] + both[pl.ds(theirs, block), :].astype(F32)


def carry_sum(exact, both):
    return pl.pallas_call(
        carry_kernel,
        out_shape=jax.ShapeDtypeStruct(exact.shape, F32),
        in_specs=[VMEM, VMEM],
        out_specs=VMEM,
        compiler_params=params(),
        name="carry",
    )(exact, both)


def shards(right_side, inverse_diag, factor_blocks, sources, counts, carry_in):
    ticks, block = right_side.shape[0], right_side.shape[1]
    groups, around = lax.axis_size("grp"), lax.axis_size("blk")
    chips = around // 2
    at = lax.axis_index("blk").astype(jnp.int32)
    odd = lax.rem(at, 2)
    chip_pairs = [[2 * c, 2 * c + 1] for c in range(chips)]
    next_pairs = [[2 * c + 1, (2 * c + 2) % around] for c in range(chips)]
    third_pairs = [[2 * c + 1, (2 * c + 4) % around] for c in range(chips)]

    def paired(value, pairs):
        return lax.all_gather(value, "blk", axis=0, tiled=True, axis_index_groups=pairs)

    def swapped(value, pairs):
        partner = [(a, b) for a, b in pairs] + [(b, a) for a, b in pairs]
        return lax.ppermute(value, "blk", partner)

    solved, own, inverse, right = first_solve(right_side, carry_in, inverse_diag)
    finished = [solved]
    seconds = [(b, (b + chips) % around) for b in range(1, around, 2)]
    for tick in range(ticks):
        if tick == 0:
            chip = paired(own, chip_pairs)
            own = jnp.where(odd == 0, chip, jnp.roll(chip, block, 0))
            held = lax.optimization_barrier((own, sources, counts, factor_blocks, inverse, right))[1:]
            kept, handed = combine(around, *held)
            given = swapped(handed, chip_pairs)
        third = swapped(own, third_pairs)[0:block]
        opposite = lax.ppermute(own, "blk", seconds)
        beside = paired(own, next_pairs)
        operands = [kept, given, own, beside, third, opposite]
        if tick + 1 == ticks:
            exact, crossing, outputs = last_sums(operands, finished)
            return (outputs, carry_sum(exact, paired(crossing, chip_pairs)))
        moved = lax.ppermute(partial_sums(operands), "grp", [(g, g + 1) for g in range(groups - 1)])
        solved, own = pair_solve(tick + 1, paired(moved, chip_pairs), right, inverse, given)
        finished.append(solved)


def solution(mesh):
    placed = (
        P(None, ("grp", "blk"), None),
        P(("grp", "blk"), None),
        P(("grp", "blk"), None, None, None),
        P(("grp", "blk"), None),
        P(("grp", "blk")),
        P(("grp", "blk"), None),
    )
    return jax.shard_map(
        shards,
        mesh=mesh,
        in_specs=placed,
        out_specs=(P(None, ("grp", "blk"), None), P(("grp", "blk"), None)),
        check_vma=False,
    )
```

```python
import functools

import jax
import jax.numpy as jnp
from jax import lax
from jax.experimental import pallas as pl
from jax.experimental.pallas import tpu as pltpu
from jax.sharding import PartitionSpec as P

F32 = jnp.float32
BF16 = jnp.bfloat16
VMEM = pl.BlockSpec(memory_space=pltpu.VMEM)
SMEM = pl.BlockSpec(memory_space=pltpu.SMEM)
HBM = pl.BlockSpec(memory_space=pltpu.HBM)
LIMIT = 20 * 1024 * 1024


def params():
    return pltpu.CompilerParams(vmem_limit_bytes=LIMIT)


def mm(a, b):
    return jnp.dot(a, b, preferred_element_type=F32)


def combine_kernel(around, count, source_list, blocks, inverse, right, chip, kept, handed, pair, source_here, landing, sums, arrived, small):
    block = inverse.shape[0]
    copy = pltpu.make_async_copy(source_list, source_here, small)
    copy.start()
    own = lax.axis_index("blk")
    second = lax.rem(own, 2)
    sign = 2 * second - 1
    pair[0:block] = chip[pl.ds(pl.multiple_of(second * block, block), block), :]
    pair[block:] = chip[pl.ds(pl.multiple_of((1 - second) * block, block), block), :]

    def copy_of(k):
        return pltpu.make_async_copy(blocks.at[0, k], landing.at[k], arrived.at[k])

    live = count[0]

    def begin(k, carry):
        copy_of(k).start()
        return carry

    lax.fori_loop(0, live, begin, 0)
    sums[...] = jnp.zeros_like(sums)
    handed[4 * block : 5 * block, :] = inverse[...]
    for tick in range(right.shape[0]):
        value = right[tick]
        high = value.astype(BF16)
        rows = pl.ds((5 + tick) * block, block)
        handed[rows, 0 : value.shape[1]] = high
        handed[rows, value.shape[1] :] = (value - high.astype(F32)).astype(BF16)
    copy.wait()

    def add(k, carry):
        copy_of(k).wait()
        offset = lax.rem(source_here[0, k] - own + 3 + around, around) - 3
        turned = offset * sign
        slot = jnp.where(k == 0, 4, jnp.where(turned >= 0, 3 - turned, 8 + turned))
        sums[slot] = sums[slot] + landing[k].astype(F32)
        return carry

    lax.fori_loop(0, live, add, 0)
    for i in range(5):
        kept[i] = sums[i].astype(BF16)
    for i in range(3):
        handed[i * block : (i + 1) * block, :] = sums[5 + i].astype(BF16)
    handed[3 * block : 4 * block, :] = sums[4].astype(BF16)


def in_hbm(value):
    return pltpu.with_memory_space_constraint(value, pltpu.HBM)


def combine(around, chip, sources, counts, factor_blocks, inverse, right):
    slots, block = factor_blocks.shape[1], factor_blocks.shape[2]
    ticks = right.shape[0]
    return pl.pallas_call(
        functools.partial(combine_kernel, around),
        out_shape=(
            jax.ShapeDtypeStruct((5, block, block), BF16),
            jax.ShapeDtypeStruct(((5 + ticks) * block, block), BF16),
            jax.ShapeDtypeStruct(chip.shape, BF16),
        ),
        in_specs=[SMEM, HBM, HBM, VMEM, VMEM, VMEM],
        out_specs=(VMEM, VMEM, VMEM),
        scratch_shapes=[
            pltpu.SMEM(sources.shape, jnp.int32),
            pltpu.VMEM((slots, block, block), BF16),
            pltpu.VMEM((8, block, block), F32),
            pltpu.SemaphoreType.DMA((slots,)),
            pltpu.SemaphoreType.DMA,
        ],
        compiler_params=params(),
        cost_estimate=pl.CostEstimate(flops=4_000_000, bytes_accessed=10_000_000, transcendentals=0),
        name="combine",
    )(counts, in_hbm(sources), in_hbm(factor_blocks), inverse, right, chip)


def first_kernel(right, incoming, inverse, solved, outgoing, inverse_here, later_here, right_here, incoming_here, arrived):
    copies = (
        pltpu.make_async_copy(right.at[0], right_here, arrived.at[0]),
        pltpu.make_async_copy(incoming, incoming_here, arrived.at[1]),
        pltpu.make_async_copy(inverse, inverse_here, arrived.at[2]),
        pltpu.make_async_copy(right.at[pl.ds(1, later_here.shape[0])], later_here, arrived.at[3]),
    )
    for copy in copies:
        copy.start()
    for copy in copies[:3]:
        copy.wait()
    value = mm(inverse_here[...], (right_here[...] - incoming_here[...]).astype(BF16))
    solved[...] = value
    outgoing[...] = value.astype(BF16)
    copies[3].wait()


def first_solve(right_side, carry_in, inverse_diag):
    ticks, block, columns = right_side.shape
    return pl.pallas_call(
        first_kernel,
        out_shape=(
            jax.ShapeDtypeStruct((block, columns), F32),
            jax.ShapeDtypeStruct((block, columns), BF16),
            jax.ShapeDtypeStruct((block, block), BF16),
            jax.ShapeDtypeStruct((ticks - 1, block, columns), F32),
        ),
        in_specs=[HBM, HBM, HBM],
        out_specs=(VMEM, VMEM, VMEM, VMEM),
        scratch_shapes=[
            pltpu.VMEM((block, columns), F32),
            pltpu.VMEM((block, columns), F32),
            pltpu.SemaphoreType.DMA((4,)),
        ],
        compiler_params=params(),
        name="first",
    )(in_hbm(right_side), in_hbm(carry_in), in_hbm(inverse_diag))


def pair_kernel(tick, both, right, inverse, given, solved, outgoing):
    block, columns = solved.shape
    odd = lax.rem(lax.axis_index("blk"), 2)
    mine = odd * (2 * block)
    theirs = (1 - odd) * (2 * block)

    def part(at):
        return both[pl.ds(pl.multiple_of(at, block), block), :].astype(F32)

    incoming = part(mine) + part(theirs + block)
    other = part(mine + block) + part(theirs)
    value = mm(inverse[...], (right[tick - 1] - incoming).astype(BF16))
    solved[...] = value
    outgoing[0:block] = value.astype(BF16)
    rows = pl.ds((4 + tick) * block, block)
    other_right = given[rows, 0:columns].astype(F32) + given[rows, columns:].astype(F32)
    value = mm(given[4 * block : 5 * block, :], (other_right - other).astype(BF16))
    outgoing[block:] = value.astype(BF16)


def pair_solve(tick, both, right, inverse, given):
    block, columns = right.shape[1:]
    operands = [both, right, inverse, given]
    return pl.pallas_call(
        functools.partial(pair_kernel, tick),
        out_shape=(
            jax.ShapeDtypeStruct((block, columns), F32),
            jax.ShapeDtypeStruct((2 * block, columns), BF16),
        ),
        in_specs=[VMEM] * len(operands),
        out_specs=(VMEM, VMEM),
        compiler_params=params(),
        name="solve",
    )(*operands)


def products(kept, given, own, beside, third, opposite):
    block = third.shape[0]
    near = lax.rem(lax.axis_index("blk"), 2) * (2 * block)

    def part(at):
        return beside[pl.ds(pl.multiple_of(at, block), block), :]

    odd_one, same_one = part(near), part(near + block)
    self_one = own[0:block]
    value = mm(kept[3], self_one)
    value += mm(kept[1], same_one)
    value += mm(kept[2], odd_one)
    value += mm(kept[0], third[...])
    value += mm(kept[4], opposite[0:block])
    other = mm(given[0:block, :], same_one)
    other += mm(given[block : 2 * block, :], odd_one)
    other += mm(given[2 * block : 3 * block, :], self_one)
    other += mm(given[3 * block : 4 * block, :], opposite[block:])
    return value, other


def partial_kernel(kept, given, own, beside, third, opposite, sums):
    block = third.shape[0]
    value, other = products(kept, given, own, beside, third, opposite)
    sums[0:block] = value.astype(BF16)
    sums[block:] = other.astype(BF16)


def last_kernel(ticks, kept, given, own, beside, third, opposite, *refs):
    solved = refs[:ticks]
    exact, sums, outputs, left = refs[ticks:]
    copies = [pltpu.make_async_copy(solved[t], outputs.at[t], left.at[t]) for t in range(ticks)]
    for copy in copies:
        copy.start()
    value, other = products(kept, given, own, beside, third, opposite)
    exact[...] = value
    sums[...] = other.astype(BF16)
    for copy in copies:
        copy.wait()


def partial_sums(operands):
    block, columns = operands[4].shape
    return pl.pallas_call(
        partial_kernel,
        out_shape=jax.ShapeDtypeStruct((2 * block, columns), BF16),
        in_specs=[VMEM] * len(operands),
        out_specs=VMEM,
        compiler_params=params(),
        name="partial",
    )(*operands)


def last_sums(operands, solved):
    block, columns = operands[4].shape
    ticks = len(solved)
    return pl.pallas_call(
        functools.partial(last_kernel, ticks),
        out_shape=(
            jax.ShapeDtypeStruct((block, columns), F32),
            jax.ShapeDtypeStruct((block, columns), BF16),
            jax.ShapeDtypeStruct((ticks, block, columns), F32),
        ),
        in_specs=[VMEM] * (len(operands) + ticks),
        out_specs=(VMEM, VMEM, HBM),
        scratch_shapes=[pltpu.SemaphoreType.DMA((ticks,))],
        compiler_params=params(),
        name="last",
    )(*operands, *solved)


def carry_kernel(exact, both, carry):
    block = exact.shape[0]
    odd = lax.rem(lax.axis_index("blk"), 2)
    theirs = pl.multiple_of((1 - odd) * block, block)
    carry[...] = exact[...] + both[pl.ds(theirs, block), :].astype(F32)


def carry_sum(exact, both):
    return pl.pallas_call(
        carry_kernel,
        out_shape=jax.ShapeDtypeStruct(exact.shape, F32),
        in_specs=[VMEM, VMEM],
        out_specs=VMEM,
        compiler_params=params(),
        name="carry",
    )(exact, both)


def shards(right_side, inverse_diag, factor_blocks, sources, counts, carry_in):
    ticks, block = right_side.shape[0], right_side.shape[1]
    groups, around = lax.axis_size("grp"), lax.axis_size("blk")
    chips = around // 2
    chip_pairs = [[2 * c, 2 * c + 1] for c in range(chips)]
    next_pairs = [[2 * c + 1, (2 * c + 2) % around] for c in range(chips)]
    third_pairs = [[2 * c + 1, (2 * c + 4) % around] for c in range(chips)]

    def paired(value, pairs):
        return lax.all_gather(value, "blk", axis=0, tiled=True, axis_index_groups=pairs)

    def swapped(value, pairs):
        partner = [(a, b) for a, b in pairs] + [(b, a) for a, b in pairs]
        return lax.ppermute(value, "blk", partner)

    solved, own, inverse, right = first_solve(right_side, carry_in, inverse_diag)
    finished = [solved]
    seconds = [(b, (b + chips) % around) for b in range(1, around, 2)]
    for tick in range(ticks):
        if tick == 0:
            chip = paired(own, chip_pairs)
            kept, handed, own = combine(around, chip, sources, counts, factor_blocks, inverse, right)
            given = swapped(handed, chip_pairs)
        third = swapped(own, third_pairs)[0:block]
        opposite = lax.ppermute(own, "blk", seconds)
        beside = paired(own, next_pairs)
        operands = [kept, given, own, beside, third, opposite]
        if tick + 1 == ticks:
            exact, crossing, outputs = last_sums(operands, finished)
            return (outputs, carry_sum(exact, paired(crossing, chip_pairs)))
        moved = lax.ppermute(partial_sums(operands), "grp", [(g, g + 1) for g in range(groups - 1)])
        solved, own = pair_solve(tick + 1, paired(moved, chip_pairs), right, inverse, given)
        finished.append(solved)


def solution(mesh):
    placed = (
        P(None, ("grp", "blk"), None),
        P(("grp", "blk"), None),
        P(("grp", "blk"), None, None, None),
        P(("grp", "blk"), None),
        P(("grp", "blk")),
        P(("grp", "blk"), None),
    )
    return jax.shard_map(
        shards,
        mesh=mesh,
        in_specs=placed,
        out_specs=(P(None, ("grp", "blk"), None), P(("grp", "blk"), None)),
        check_vma=False,
    )
```

```python
import functools

import jax
import jax.numpy as jnp
from jax import lax
from jax.experimental import pallas as pl
from jax.experimental.pallas import tpu as pltpu
from jax.sharding import PartitionSpec as P

F32 = jnp.float32
BF16 = jnp.bfloat16
VMEM = pl.BlockSpec(memory_space=pltpu.VMEM)
SMEM = pl.BlockSpec(memory_space=pltpu.SMEM)
HBM = pl.BlockSpec(memory_space=pltpu.HBM)
LIMIT = 20 * 1024 * 1024


def params():
    return pltpu.CompilerParams(vmem_limit_bytes=LIMIT)


def mm(a, b):
    return jnp.dot(a, b, preferred_element_type=F32)


def combine_kernel(around, count, source_list, blocks, inverse, right, chip, kept, handed, pair, source_here, landing, sums, arrived, small):
    block = inverse.shape[0]
    copy = pltpu.make_async_copy(source_list, source_here, small)
    copy.start()
    own = lax.axis_index("blk")
    second = lax.rem(own, 2)
    sign = 2 * second - 1
    pair[0:block] = chip[pl.ds(pl.multiple_of(second * block, block), block), :]
    pair[block:] = chip[pl.ds(pl.multiple_of((1 - second) * block, block), block), :]

    def copy_of(k):
        return pltpu.make_async_copy(blocks.at[0, k], landing.at[k], arrived.at[k])

    live = count[0]

    def begin(k, carry):
        copy_of(k).start()
        return carry

    lax.fori_loop(0, live, begin, 0)
    sums[...] = jnp.zeros_like(sums)
    handed[4 * block : 5 * block, :] = inverse[...]
    for tick in range(right.shape[0]):
        value = right[tick]
        high = value.astype(BF16)
        rows = pl.ds((5 + tick) * block, block)
        handed[rows, 0 : value.shape[1]] = high
        handed[rows, value.shape[1] :] = (value - high.astype(F32)).astype(BF16)
    copy.wait()

    def add(k, carry):
        copy_of(k).wait()
        offset = lax.rem(source_here[0, k] - own + 3 + around, around) - 3
        turned = offset * sign
        slot = jnp.where(k == 0, 4, jnp.where(turned >= 0, 3 - turned, 8 + turned))
        sums[slot] = sums[slot] + landing[k].astype(F32)
        return carry

    lax.fori_loop(0, live, add, 0)
    for i in range(5):
        kept[i] = sums[i].astype(BF16)
    for i in range(3):
        handed[i * block : (i + 1) * block, :] = sums[5 + i].astype(BF16)
    handed[3 * block : 4 * block, :] = sums[4].astype(BF16)


def in_hbm(value):
    return pltpu.with_memory_space_constraint(value, pltpu.HBM)


def combine(around, chip, sources, counts, factor_blocks, inverse, right):
    slots, block = factor_blocks.shape[1], factor_blocks.shape[2]
    ticks = right.shape[0]
    return pl.pallas_call(
        functools.partial(combine_kernel, around),
        out_shape=(
            jax.ShapeDtypeStruct((5, block, block), BF16),
            jax.ShapeDtypeStruct(((5 + ticks) * block, block), BF16),
            jax.ShapeDtypeStruct(chip.shape, BF16),
        ),
        in_specs=[SMEM, HBM, HBM, VMEM, VMEM, VMEM],
        out_specs=(VMEM, VMEM, VMEM),
        scratch_shapes=[
            pltpu.SMEM(sources.shape, jnp.int32),
            pltpu.VMEM((slots, block, block), BF16),
            pltpu.VMEM((8, block, block), F32),
            pltpu.SemaphoreType.DMA((slots,)),
            pltpu.SemaphoreType.DMA,
        ],
        compiler_params=params(),
        cost_estimate=pl.CostEstimate(flops=4_000_000, bytes_accessed=10_000_000, transcendentals=0),
        name="combine",
    )(counts, in_hbm(sources), in_hbm(factor_blocks), inverse, right, chip)


def first_kernel(right, incoming, inverse, solved, outgoing, inverse_here, later_here, right_here, incoming_here, arrived):
    copies = (
        pltpu.make_async_copy(right.at[0], right_here, arrived.at[0]),
        pltpu.make_async_copy(incoming, incoming_here, arrived.at[1]),
        pltpu.make_async_copy(inverse, inverse_here, arrived.at[2]),
        pltpu.make_async_copy(right.at[pl.ds(1, later_here.shape[0])], later_here, arrived.at[3]),
    )
    for copy in copies:
        copy.start()
    for copy in copies[:3]:
        copy.wait()
    value = mm(inverse_here[...], (right_here[...] - incoming_here[...]).astype(BF16))
    solved[...] = value
    outgoing[...] = value.astype(BF16)
    copies[3].wait()


def first_solve(right_side, carry_in, inverse_diag):
    ticks, block, columns = right_side.shape
    return pl.pallas_call(
        first_kernel,
        out_shape=(
            jax.ShapeDtypeStruct((block, columns), F32),
            jax.ShapeDtypeStruct((block, columns), BF16),
            jax.ShapeDtypeStruct((block, block), BF16),
            jax.ShapeDtypeStruct((ticks - 1, block, columns), F32),
        ),
        in_specs=[HBM, HBM, HBM],
        out_specs=(VMEM, VMEM, VMEM, VMEM),
        scratch_shapes=[
            pltpu.VMEM((block, columns), F32),
            pltpu.VMEM((block, columns), F32),
            pltpu.SemaphoreType.DMA((4,)),
        ],
        compiler_params=params(),
        name="first",
    )(in_hbm(right_side), in_hbm(carry_in), in_hbm(inverse_diag))


def pair_kernel(tick, both, right, inverse, given, solved, outgoing):
    block, columns = solved.shape
    odd = lax.rem(lax.axis_index("blk"), 2)
    mine = odd * (2 * block)
    theirs = (1 - odd) * (2 * block)

    def part(at):
        return both[pl.ds(pl.multiple_of(at, block), block), :].astype(F32)

    incoming = part(mine) + part(theirs + block)
    other = part(mine + block) + part(theirs)
    value = mm(inverse[...], (right[tick - 1] - incoming).astype(BF16))
    solved[...] = value
    outgoing[0:block] = value.astype(BF16)
    rows = pl.ds((4 + tick) * block, block)
    other_right = given[rows, 0:columns].astype(F32) + given[rows, columns:].astype(F32)
    value = mm(given[4 * block : 5 * block, :], (other_right - other).astype(BF16))
    outgoing[block:] = value.astype(BF16)


def pair_solve(tick, both, right, inverse, given):
    block, columns = right.shape[1:]
    operands = [both, right, inverse, given]
    return pl.pallas_call(
        functools.partial(pair_kernel, tick),
        out_shape=(
            jax.ShapeDtypeStruct((block, columns), F32),
            jax.ShapeDtypeStruct((2 * block, columns), BF16),
        ),
        in_specs=[VMEM] * len(operands),
        out_specs=(VMEM, VMEM),
        compiler_params=params(),
        name="solve",
    )(*operands)


def products(kept, given, own, beside, third, opposite):
    block = beside.shape[0] // 2
    there = pl.multiple_of(lax.rem(lax.axis_index("blk"), 2) * block, block)
    odd_one, same_one = beside[0:block], beside[block:]
    self_one = own[0:block]
    value = mm(kept[3], self_one)
    value += mm(kept[1], same_one)
    value += mm(kept[2], odd_one)
    value += mm(kept[0], third[pl.ds(there, block), :])
    value += mm(kept[4], opposite[0:block])
    other = mm(given[0:block, :], same_one)
    other += mm(given[block : 2 * block, :], odd_one)
    other += mm(given[2 * block : 3 * block, :], self_one)
    other += mm(given[3 * block : 4 * block, :], opposite[block:])
    return value, other


def partial_kernel(kept, given, own, beside, third, opposite, sums):
    block = beside.shape[0] // 2
    value, other = products(kept, given, own, beside, third, opposite)
    sums[0:block] = value.astype(BF16)
    sums[block:] = other.astype(BF16)


def last_kernel(ticks, kept, given, own, beside, third, opposite, *refs):
    solved = refs[:ticks]
    exact, sums, outputs, left = refs[ticks:]
    copies = [pltpu.make_async_copy(solved[t], outputs.at[t], left.at[t]) for t in range(ticks)]
    for copy in copies:
        copy.start()
    value, other = products(kept, given, own, beside, third, opposite)
    exact[...] = value
    sums[...] = other.astype(BF16)
    for copy in copies:
        copy.wait()


def partial_sums(operands):
    block, columns = operands[4].shape[0] // 2, operands[4].shape[1]
    return pl.pallas_call(
        partial_kernel,
        out_shape=jax.ShapeDtypeStruct((2 * block, columns), BF16),
        in_specs=[VMEM] * len(operands),
        out_specs=VMEM,
        compiler_params=params(),
        name="partial",
    )(*operands)


def last_sums(operands, solved):
    block, columns = operands[4].shape[0] // 2, operands[4].shape[1]
    ticks = len(solved)
    return pl.pallas_call(
        functools.partial(last_kernel, ticks),
        out_shape=(
            jax.ShapeDtypeStruct((block, columns), F32),
            jax.ShapeDtypeStruct((block, columns), BF16),
            jax.ShapeDtypeStruct((ticks, block, columns), F32),
        ),
        in_specs=[VMEM] * (len(operands) + ticks),
        out_specs=(VMEM, VMEM, HBM),
        scratch_shapes=[pltpu.SemaphoreType.DMA((ticks,))],
        compiler_params=params(),
        name="last",
    )(*operands, *solved)


def carry_kernel(exact, both, carry):
    block = exact.shape[0]
    odd = lax.rem(lax.axis_index("blk"), 2)
    theirs = pl.multiple_of((1 - odd) * block, block)
    carry[...] = exact[...] + both[pl.ds(theirs, block), :].astype(F32)


def carry_sum(exact, both):
    return pl.pallas_call(
        carry_kernel,
        out_shape=jax.ShapeDtypeStruct(exact.shape, F32),
        in_specs=[VMEM, VMEM],
        out_specs=VMEM,
        compiler_params=params(),
        name="carry",
    )(exact, both)


def shards(right_side, inverse_diag, factor_blocks, sources, counts, carry_in):
    ticks, block = right_side.shape[0], right_side.shape[1]
    groups, around = lax.axis_size("grp"), lax.axis_size("blk")
    chips = around // 2
    chip_pairs = [[2 * c, 2 * c + 1] for c in range(chips)]
    next_pairs = [[2 * c + 1, (2 * c + 2) % around] for c in range(chips)]
    third_pairs = [[2 * c + 1, (2 * c + 4) % around] for c in range(chips)]

    def paired(value, pairs):
        return lax.all_gather(value, "blk", axis=0, tiled=True, axis_index_groups=pairs)

    def swapped(value, pairs):
        partner = [(a, b) for a, b in pairs] + [(b, a) for a, b in pairs]
        return lax.ppermute(value, "blk", partner)

    solved, own, inverse, right = first_solve(right_side, carry_in, inverse_diag)
    finished = [solved]
    seconds = [(b, (b + chips) % around) for b in range(1, around, 2)]
    for tick in range(ticks):
        if tick == 0:
            chip = paired(own, chip_pairs)
            kept, handed, own = combine(around, chip, sources, counts, factor_blocks, inverse, right)
            given = swapped(handed, chip_pairs)
        beside = swapped(own, next_pairs)
        opposite = lax.ppermute(own, "blk", seconds)
        third = paired(own[0:block], third_pairs)
        operands = [kept, given, own, beside, third, opposite]
        if tick + 1 == ticks:
            exact, crossing, outputs = last_sums(operands, finished)
            return (outputs, carry_sum(exact, paired(crossing, chip_pairs)))
        moved = lax.ppermute(partial_sums(operands), "grp", [(g, g + 1) for g in range(groups - 1)])
        solved, own = pair_solve(tick + 1, paired(moved, chip_pairs), right, inverse, given)
        finished.append(solved)


def solution(mesh):
    placed = (
        P(None, ("grp", "blk"), None),
        P(("grp", "blk"), None),
        P(("grp", "blk"), None, None, None),
        P(("grp", "blk"), None),
        P(("grp", "blk")),
        P(("grp", "blk"), None),
    )
    return jax.shard_map(
        shards,
        mesh=mesh,
        in_specs=placed,
        out_specs=(P(None, ("grp", "blk"), None), P(("grp", "blk"), None)),
        check_vma=False,
    )
```

```python
import functools

import jax
import jax.numpy as jnp
from jax import lax
from jax.experimental import pallas as pl
from jax.experimental.pallas import tpu as pltpu
from jax.sharding import PartitionSpec as P

F32 = jnp.float32
BF16 = jnp.bfloat16
VMEM = pl.BlockSpec(memory_space=pltpu.VMEM)
SMEM = pl.BlockSpec(memory_space=pltpu.SMEM)
HBM = pl.BlockSpec(memory_space=pltpu.HBM)
LIMIT = 20 * 1024 * 1024


def params():
    return pltpu.CompilerParams(vmem_limit_bytes=LIMIT)


def mm(a, b):
    return jnp.dot(a, b, preferred_element_type=F32)


def first_kernel(
    around, count, source_list, blocks, right, incoming, inverse,
    solved, outgoing, inverse_here, later, kept, handed,
    right_here, incoming_here, source_here, landing, sums, arrived, small,
):
    block = inverse_here.shape[0]
    live = count[0]
    copies = (
        pltpu.make_async_copy(right.at[0], right_here, small.at[0]),
        pltpu.make_async_copy(incoming, incoming_here, small.at[1]),
        pltpu.make_async_copy(inverse, inverse_here, small.at[2]),
        pltpu.make_async_copy(right.at[pl.ds(1, later.shape[0])], later, small.at[3]),
        pltpu.make_async_copy(source_list, source_here, small.at[4]),
    )
    for copy in copies:
        copy.start()

    def copy_of(k):
        return pltpu.make_async_copy(blocks.at[0, k], landing.at[k], arrived.at[k])

    def begin(k, carry):
        copy_of(k).start()
        return carry

    lax.fori_loop(0, live, begin, 0)
    sums[...] = jnp.zeros_like(sums)
    own = lax.axis_index("blk")
    sign = 2 * lax.rem(own, 2) - 1
    for copy in copies[:3]:
        copy.wait()
    value = mm(inverse_here[...], (right_here[...] - incoming_here[...]).astype(BF16))
    solved[...] = value
    outgoing[...] = value.astype(BF16)
    handed[4 * block : 5 * block, :] = inverse_here[...]
    for copy in copies[3:]:
        copy.wait()
    for tick in range(later.shape[0]):
        value = later[tick]
        high = value.astype(BF16)
        rows = pl.ds((5 + tick) * block, block)
        handed[rows, 0 : value.shape[1]] = high
        handed[rows, value.shape[1] :] = (value - high.astype(F32)).astype(BF16)

    def add(k, carry):
        copy_of(k).wait()
        offset = lax.rem(source_here[0, k] - own + 3 + around, around) - 3
        turned = offset * sign
        slot = jnp.where(k == 0, 4, jnp.where(turned >= 0, 3 - turned, 8 + turned))
        sums[slot] = sums[slot] + landing[k].astype(F32)
        return carry

    lax.fori_loop(0, live, add, 0)
    for i in range(5):
        kept[i] = sums[i].astype(BF16)
    for i in range(3):
        handed[i * block : (i + 1) * block, :] = sums[5 + i].astype(BF16)
    handed[3 * block : 4 * block, :] = sums[4].astype(BF16)


def in_hbm(value):
    return pltpu.with_memory_space_constraint(value, pltpu.HBM)


def first_solve(around, sources, counts, factor_blocks, right_side, carry_in, inverse_diag):
    slots = factor_blocks.shape[1]
    ticks, block, columns = right_side.shape
    return pl.pallas_call(
        functools.partial(first_kernel, around),
        out_shape=(
            jax.ShapeDtypeStruct((block, columns), F32),
            jax.ShapeDtypeStruct((block, columns), BF16),
            jax.ShapeDtypeStruct((block, block), BF16),
            jax.ShapeDtypeStruct((ticks - 1, block, columns), F32),
            jax.ShapeDtypeStruct((5, block, block), BF16),
            jax.ShapeDtypeStruct(((4 + ticks) * block, block), BF16),
        ),
        in_specs=[SMEM, HBM, HBM, HBM, HBM, HBM],
        out_specs=(VMEM,) * 6,
        scratch_shapes=[
            pltpu.VMEM((block, columns), F32),
            pltpu.VMEM((block, columns), F32),
            pltpu.SMEM(sources.shape, jnp.int32),
            pltpu.VMEM((slots, block, block), BF16),
            pltpu.VMEM((8, block, block), F32),
            pltpu.SemaphoreType.DMA((slots,)),
            pltpu.SemaphoreType.DMA((5,)),
        ],
        compiler_params=params(),
        name="first",
    )(counts, *(in_hbm(a) for a in (sources, factor_blocks, right_side, carry_in, inverse_diag)))


def pair_kernel(tick, both, right, inverse, given, solved, outgoing):
    block, columns = solved.shape
    odd = lax.rem(lax.axis_index("blk"), 2)
    mine = odd * (2 * block)
    theirs = (1 - odd) * (2 * block)

    def part(at):
        return both[pl.ds(pl.multiple_of(at, block), block), :].astype(F32)

    incoming = part(mine) + part(theirs + block)
    other = part(mine + block) + part(theirs)
    value = mm(inverse[...], (right[tick - 1] - incoming).astype(BF16))
    solved[...] = value
    outgoing[0:block] = value.astype(BF16)
    rows = pl.ds((4 + tick) * block, block)
    other_right = given[rows, 0:columns].astype(F32) + given[rows, columns:].astype(F32)
    value = mm(given[4 * block : 5 * block, :], (other_right - other).astype(BF16))
    outgoing[block:] = value.astype(BF16)


def pair_solve(tick, both, right, inverse, given):
    block, columns = right.shape[1:]
    operands = [both, right, inverse, given]
    return pl.pallas_call(
        functools.partial(pair_kernel, tick),
        out_shape=(
            jax.ShapeDtypeStruct((block, columns), F32),
            jax.ShapeDtypeStruct((2 * block, columns), BF16),
        ),
        in_specs=[VMEM] * len(operands),
        out_specs=(VMEM, VMEM),
        compiler_params=params(),
        name="solve",
    )(*operands)


def products(kept, given, own, beside, third, opposite):
    block = beside.shape[0] // 2
    there = pl.multiple_of(lax.rem(lax.axis_index("blk"), 2) * block, block)
    odd_one, same_one = beside[0:block], beside[block:]
    self_one = own[0:block]
    value = mm(kept[3], self_one)
    value += mm(kept[1], same_one)
    value += mm(kept[2], odd_one)
    value += mm(kept[0], third[pl.ds(there, block), :])
    value += mm(kept[4], opposite[0:block])
    other = mm(given[0:block, :], same_one)
    other += mm(given[block : 2 * block, :], odd_one)
    other += mm(given[2 * block : 3 * block, :], self_one)
    other += mm(given[3 * block : 4 * block, :], opposite[block:])
    return value, other


def partial_kernel(kept, given, own, beside, third, opposite, sums):
    block = beside.shape[0] // 2
    value, other = products(kept, given, own, beside, third, opposite)
    sums[0:block] = value.astype(BF16)
    sums[block:] = other.astype(BF16)


def last_kernel(ticks, kept, given, own, beside, third, opposite, *refs):
    solved = refs[:ticks]
    exact, sums, outputs, left = refs[ticks:]
    copies = [pltpu.make_async_copy(solved[t], outputs.at[t], left.at[t]) for t in range(ticks)]
    for copy in copies:
        copy.start()
    value, other = products(kept, given, own, beside, third, opposite)
    exact[...] = value
    sums[...] = other.astype(BF16)
    for copy in copies:
        copy.wait()


def partial_sums(operands):
    block, columns = operands[4].shape[0] // 2, operands[4].shape[1]
    return pl.pallas_call(
        partial_kernel,
        out_shape=jax.ShapeDtypeStruct((2 * block, columns), BF16),
        in_specs=[VMEM] * len(operands),
        out_specs=VMEM,
        compiler_params=params(),
        name="partial",
    )(*operands)


def last_sums(operands, solved):
    block, columns = operands[4].shape[0] // 2, operands[4].shape[1]
    ticks = len(solved)
    return pl.pallas_call(
        functools.partial(last_kernel, ticks),
        out_shape=(
            jax.ShapeDtypeStruct((block, columns), F32),
            jax.ShapeDtypeStruct((block, columns), BF16),
            jax.ShapeDtypeStruct((ticks, block, columns), F32),
        ),
        in_specs=[VMEM] * (len(operands) + ticks),
        out_specs=(VMEM, VMEM, HBM),
        scratch_shapes=[pltpu.SemaphoreType.DMA((ticks,))],
        compiler_params=params(),
        name="last",
    )(*operands, *solved)


def carry_kernel(exact, both, carry):
    block = exact.shape[0]
    odd = lax.rem(lax.axis_index("blk"), 2)
    theirs = pl.multiple_of((1 - odd) * block, block)
    carry[...] = exact[...] + both[pl.ds(theirs, block), :].astype(F32)


def carry_sum(exact, both):
    return pl.pallas_call(
        carry_kernel,
        out_shape=jax.ShapeDtypeStruct(exact.shape, F32),
        in_specs=[VMEM, VMEM],
        out_specs=VMEM,
        compiler_params=params(),
        name="carry",
    )(exact, both)


def shards(right_side, inverse_diag, factor_blocks, sources, counts, carry_in):
    ticks, block = right_side.shape[0], right_side.shape[1]
    groups, around = lax.axis_size("grp"), lax.axis_size("blk")
    chips = around // 2
    chip_pairs = [[2 * c, 2 * c + 1] for c in range(chips)]
    next_pairs = [[2 * c + 1, (2 * c + 2) % around] for c in range(chips)]
    third_pairs = [[2 * c + 1, (2 * c + 4) % around] for c in range(chips)]

    def paired(value, pairs):
        return lax.all_gather(value, "blk", axis=0, tiled=True, axis_index_groups=pairs)

    def swapped(value, pairs):
        partner = [(a, b) for a, b in pairs] + [(b, a) for a, b in pairs]
        return lax.ppermute(value, "blk", partner)

    solved, own, inverse, right, kept, handed = first_solve(
        around, sources, counts, factor_blocks, right_side, carry_in, inverse_diag
    )
    finished = [solved]
    seconds = [(b, (b + chips) % around) for b in range(1, around, 2)]
    for tick in range(ticks):
        if tick == 0:
            chip = paired(own, chip_pairs)
            second = lax.rem(lax.axis_index("blk"), 2)
            own = jnp.where(second == 0, chip, jnp.roll(chip, block, 0))
            given = swapped(handed, chip_pairs)
        beside = swapped(own, next_pairs)
        opposite = lax.ppermute(own, "blk", seconds)
        third = paired(own[0:block], third_pairs)
        operands = [kept, given, own, beside, third, opposite]
        if tick + 1 == ticks:
            exact, crossing, outputs = last_sums(operands, finished)
            return (outputs, carry_sum(exact, paired(crossing, chip_pairs)))
        moved = lax.ppermute(partial_sums(operands), "grp", [(g, g + 1) for g in range(groups - 1)])
        solved, own = pair_solve(tick + 1, paired(moved, chip_pairs), right, inverse, given)
        finished.append(solved)


def solution(mesh):
    placed = (
        P(None, ("grp", "blk"), None),
        P(("grp", "blk"), None),
        P(("grp", "blk"), None, None, None),
        P(("grp", "blk"), None),
        P(("grp", "blk")),
        P(("grp", "blk"), None),
    )
    return jax.shard_map(
        shards,
        mesh=mesh,
        in_specs=placed,
        out_specs=(P(None, ("grp", "blk"), None), P(("grp", "blk"), None)),
        check_vma=False,
    )
```
